256 devices in a mesh: row: 16 (over y, x_lo, core), col: 16 (over z, x_hi).
Axes of the slice: x: 4 (x_hi: 2, x_lo: 2; x = x_hi * 2 + x_lo), y: 4, z: 8, core: 2. Of those that a mesh axis runs over, the one named last changes fastest.
Arguments:
- features: bfloat16 [32768, 1024], P(('row', 'col')), may hold values from -6 to 6
- node_valid: int32 [256, 128], P(('row', 'col')), may hold values 0 or 1
- self_mask: int32 [256, 128, 128], P(('row', 'col')), may hold values 0 or 1
- pair_blocks: int32 [16, 16, 8, 2], P('row', 'col'), may hold values from 0 to 255, as said below
- pair_count: int32 [16, 16], P('row', 'col'), may hold values from 0 to 8, as said below
- pair_masks: int32 [16, 16, 8, 128, 128], P('row', 'col'), may hold values 0 or 1
- weight_src: bfloat16 [1024, 1024], replicated, may hold values from -0.1875 to 0.1875
- weight_tgt: bfloat16 [1024, 1024], replicated, may hold values from -0.1875 to 0.1875
- attn: float32 [4, 256], replicated
- bias: float32 [1024], replicated, may hold values from -6 to 6
Outputs:
- attended: bfloat16 [32768, 1024], P(('row', 'col'))
The draws below stay inside these ranges and needn't reach their ends.
Inputs may be any that keep to these rules, and one draw needn't show every extreme that they name: `pair_blocks`: cell (r, c) lists in each slot a pair (i, j) of different blocks: i is held by a device of grid row r and j by a device of grid column c, block b being held by device b // 1 counted row by row. No unordered pair stands in two live slots. Slots from pair_count on are not used. Some cell has all 8 slots live.
All inputs are finite; a program needn't handle non-finite values. No bound on the sum of `node_valid` or of `self_mask` or of `pair_masks` on one device may be relied on, other than what follows from the above.
Results may differ from the reference program's by a relative error of at most 0.012.
The reference program's roundings to bfloat16 on the way (of `source`, `target` and `weights`) count: a program that leaves them out, or rounds other values in their place, can miss the bound.
Values may be sent and summed in bfloat16 or wider, within the bound.
No kernel may reach another device: no remote copies, remote signals or barrier semaphores. Data moves between devices by JAX's collectives and lax.ppermute only.
A program may use at most 128 MiB of HBM per device.

```python
import math
import jax
import jax.numpy as jnp
from jax import lax

D = 1024
H = 4
HS = 256
BS = 128
CELL_CAPACITY = 8
BLK = 1
NB = 256
NODES = 32768
N_ROW = 16
N_COL = 16


def pair_table(key):
    starting_index = jax.random.fold_in(key, 4099)
    selection_seed, tally_seed, clumping_seed = jax.random.split(starting_index, 3)
    span_row = N_COL * BLK
    span_col = N_ROW * BLK
    total = span_row * span_col
    grid_rows = jnp.arange(N_ROW, dtype=jnp.int32).reshape(N_ROW, 1, 1, 1)
    grid_cols = jnp.arange(N_COL, dtype=jnp.int32).reshape(1, N_COL, 1, 1)
    row_slot = jnp.arange(span_row, dtype=jnp.int32).reshape(1, 1, span_row, 1)
    col_slot = jnp.arange(span_col, dtype=jnp.int32).reshape(1, 1, 1, span_col)
    shape = (N_ROW, N_COL, span_row, span_col)
    first = jnp.broadcast_to(grid_rows * span_row + row_slot, shape).reshape(N_ROW, N_COL, total)
    second = jnp.broadcast_to((col_slot // BLK * N_COL + grid_cols) * BLK + col_slot % BLK, shape).reshape(N_ROW, N_COL, total)
    allowed = (first != second) & ((first < second) != ((first + second) % 2 == 1))
    noise = jax.random.randint(selection_seed, (N_ROW, N_COL, total), 0, 16384, dtype=jnp.int32)
    ranking = noise * total + jnp.arange(total, dtype=jnp.int32) + allowed.astype(jnp.int32) * (1 << 30)
    ranked, picked = lax.top_k(ranking, CELL_CAPACITY)
    first_pick = jnp.take_along_axis(first, picked, axis=2)
    second_pick = jnp.take_along_axis(second, picked, axis=2)
    listed = jnp.stack([first_pick, second_pick], axis=-1).astype(jnp.int32)
    room = jnp.sum(allowed.astype(jnp.int32), axis=2)
    couple_tallies = jax.random.randint(tally_seed, (N_ROW, N_COL), 0, 5, dtype=jnp.int32)
    clustered_couples = jax.random.randint(clumping_seed, (N_ROW, N_COL), 0, 8, dtype=jnp.int32) == 0
    couple_tallies = jnp.where(clustered_couples, CELL_CAPACITY, couple_tallies)
    couple_tallies = couple_tallies.at[0, 0].set(CELL_CAPACITY)
    couple_tallies = jnp.minimum(couple_tallies, room).astype(jnp.int32)
    return (listed, couple_tallies)


def draw_pair_blocks(key, part):
    listed, couple_tallies = pair_table(key)
    return listed


def draw_pair_count(key, part):
    listed, couple_tallies = pair_table(key)
    return couple_tallies


def draw_attn(key, part):
    values = jax.random.normal(jax.random.fold_in(key, 11), (H, HS), jnp.float32) * (2.0 / math.sqrt(HS))
    return values


def place_ends(values, key, smallest, high):
    index_at = [jax.random.randint(jax.random.fold_in(key, axis), (), 0, length) for axis, length in enumerate(values.shape)]
    longest = values.shape.index(max(values.shape))
    beside = index_at[:longest] + [(index_at[longest] + 1) % values.shape[longest]] + index_at[longest + 1:]
    return values.at[tuple(index_at)].set(smallest).at[tuple(beside)].set(high)


def level_of(stream_key, extent, cuts, low, largest):
    def one(axis_at, blocks):
        heights = jax.random.uniform(jax.random.fold_in(jax.random.fold_in(stream_key, 6), axis_at), (blocks,), jnp.float32, low / len(cuts), largest / len(cuts))
        return jnp.repeat(jnp.exp(heights), extent[axis_at] // blocks).reshape((-1,) + (1,) * (len(extent) - axis_at - 1))

    factor_of = one(*cuts[0])
    for cut in cuts[1:]:
        factor_of = factor_of * one(*cut)
    return factor_of


def centred(own_key, shape, scale, most, cuts=(), kind=jnp.bfloat16):
    values = jax.random.normal(own_key, shape, jnp.float32) * scale
    if len(cuts) > 0:
        values = level_of(own_key, shape, cuts, -0.22, 0.18) * values
    return jnp.clip(values, min=-most, max=most).astype(kind)


def setup_inputs(seed: int = 0) -> dict:
    key_of = jax.random.split(jax.random.key(seed), 11)
    return {
        "features": centred(key_of[0], (NODES, D), 1.0, 6.0, ((0, 256),)),
        "node_valid": place_ends((jax.random.randint(key_of[1], (NB, BS), 0, 8) < 7).astype(jnp.int32), jax.random.fold_in(key_of[1], 1), 0, 1),
        "self_mask": place_ends((jax.random.randint(key_of[2], (NB, BS, BS), 0, 8) < 1).astype(jnp.int32), jax.random.fold_in(key_of[2], 1), 0, 1),
        "pair_blocks": draw_pair_blocks(jax.random.fold_in(key_of[10], 71), 0),
        "pair_count": draw_pair_count(jax.random.fold_in(key_of[10], 71), 0),
        "pair_masks": place_ends((jax.random.randint(key_of[5], (N_ROW, N_COL, CELL_CAPACITY, BS, BS), 0, 8) < 1).astype(jnp.int32), jax.random.fold_in(key_of[5], 1), 0, 1),
        "weight_src": centred(key_of[6], (D, D), D ** -0.5, 0.1875),
        "weight_tgt": centred(key_of[7], (D, D), D ** -0.5, 0.1875),
        "attn": draw_attn(jax.random.fold_in(key_of[10], 71), 0),
        "bias": centred(key_of[9], (D,), 1.0, 6.0, (), jnp.float32),
    }


FLOOR = -1.0e30


def score_block(target, source, attn):
    heads = attn.shape[0]
    head_width = attn.shape[1]
    target_heads = target.reshape(target.shape[0], heads, head_width)
    source_heads = source.reshape(source.shape[0], heads, head_width)
    planes = []
    for head in range(heads):
        mixed = target_heads[:, head, :].astype(jnp.float32)[:, None, :] + source_heads[:, head, :].astype(jnp.float32)[None, :, :]
        planes.append(jnp.sum(jax.nn.leaky_relu(mixed, 0.2) * attn[head], axis=-1))
    return jnp.stack(planes)


def weigh(weights, source, heads):
    nodes = source.shape[0]
    source_heads = source.reshape(nodes, heads, source.shape[1] // heads).astype(jnp.float32)
    rounded = weights.astype(jnp.bfloat16).astype(jnp.float32)
    mixed = jnp.einsum("hts,shd->thd", rounded, source_heads, precision=lax.Precision.HIGHEST)
    return mixed.reshape(weights.shape[1], source.shape[1])


def to_wire(value):
    return lax.optimization_barrier(value.astype(jnp.bfloat16)).astype(jnp.float32)


def reference(features, node_valid, self_mask, pair_blocks, pair_count, pair_masks, weight_src, weight_tgt, attn, bias):
    blocks = node_valid.shape[0]
    block_size = node_valid.shape[1]
    width = features.shape[1]
    heads = attn.shape[0]
    head_width = attn.shape[1]
    source_all = jnp.dot(features, weight_src, preferred_element_type=jnp.float32).astype(jnp.bfloat16).reshape(blocks, block_size, width)
    target_all = jnp.dot(features, weight_tgt, preferred_element_type=jnp.float32).astype(jnp.bfloat16).reshape(blocks, block_size, width)
    valid = node_valid > 0
    span_row = N_COL * BLK
    span_col = N_ROW * BLK
    flat_blocks = pair_blocks.reshape(-1, 2)
    flat_masks = pair_masks.reshape(-1, block_size, block_size)
    slot_ids = jnp.arange(CELL_CAPACITY, dtype=jnp.int32)
    live = (slot_ids[None, None, :] < pair_count[:, :, None]).reshape(-1)

    def both(item):
        first = flat_blocks[item, 0]
        second = flat_blocks[item, 1]
        adjacency = (flat_masks[item] > 0) & valid[first][:, None] & valid[second][None, :]
        forward = jnp.where(adjacency[None], score_block(target_all[first], source_all[second], attn), FLOOR)
        backward = jnp.where(adjacency.T[None], score_block(target_all[second], source_all[first], attn), FLOOR)
        return first, second, adjacency, forward, backward

    def max_pass(item, carry):
        def live_step(state):
            first, second, adjacency, forward, backward = both(item)
            return (state[0].at[first].max(jnp.max(forward, axis=-1)), state[1].at[second].max(jnp.max(backward, axis=-1)))
        return lax.cond(live[item], live_step, lambda state: state, carry)

    start_peak = jnp.full((blocks, heads, block_size), FLOOR, jnp.float32)
    row_peak, col_peak = lax.fori_loop(0, flat_blocks.shape[0], max_pass, (start_peak, start_peak))

    def cell_pass(cell, totals):
        grid_row = cell // N_COL
        grid_col = cell % N_COL

        def slot_pass(slot, parts):
            item = cell * CELL_CAPACITY + slot

            def live_step(state):
                first, second, adjacency, forward, backward = both(item)
                row_slot = first - grid_row * span_row
                col_slot = (second // BLK) // N_COL * BLK + second % BLK
                weights_fwd = jnp.where(adjacency[None], jnp.exp(forward - row_peak[first][:, :, None]), 0.0)
                weights_bwd = jnp.where(adjacency.T[None], jnp.exp(backward - col_peak[second][:, :, None]), 0.0)
                numer_fwd = weigh(weights_fwd, source_all[second], heads)
                numer_bwd = weigh(weights_bwd, source_all[first], heads)
                return (state[0].at[row_slot].add(numer_fwd), state[1].at[row_slot].add(jnp.sum(weights_fwd, axis=-1)),
                        state[2].at[col_slot].add(numer_bwd), state[3].at[col_slot].add(jnp.sum(weights_bwd, axis=-1)))
            return lax.cond(live[item], live_step, lambda state: state, parts)

        parts = (jnp.zeros((span_row, block_size, width), jnp.float32), jnp.zeros((span_row, heads, block_size), jnp.float32),
                 jnp.zeros((span_col, block_size, width), jnp.float32), jnp.zeros((span_col, heads, block_size), jnp.float32))
        parts = lax.fori_loop(0, CELL_CAPACITY, slot_pass, parts)
        row_numer = totals[0].at[grid_row].add(to_wire(parts[0]).reshape(N_COL, BLK, block_size, width))
        row_denom = totals[1].at[grid_row].add(to_wire(parts[1]).reshape(N_COL, BLK, heads, block_size))
        col_numer = totals[2].at[:, grid_col].add(to_wire(parts[2]).reshape(N_ROW, BLK, block_size, width))
        col_denom = totals[3].at[:, grid_col].add(to_wire(parts[3]).reshape(N_ROW, BLK, heads, block_size))
        return (row_numer, row_denom, col_numer, col_denom)

    totals = (jnp.zeros((N_ROW, N_COL, BLK, block_size, width), jnp.float32), jnp.zeros((N_ROW, N_COL, BLK, heads, block_size), jnp.float32),
              jnp.zeros((N_ROW, N_COL, BLK, block_size, width), jnp.float32), jnp.zeros((N_ROW, N_COL, BLK, heads, block_size), jnp.float32))
    totals = lax.fori_loop(0, N_ROW * N_COL, cell_pass, totals)
    row_numer = totals[0].reshape(blocks, block_size, width)
    row_denom = totals[1].reshape(blocks, heads, block_size)
    col_numer = totals[2].reshape(blocks, block_size, width)
    col_denom = totals[3].reshape(blocks, heads, block_size)
    identity = jnp.eye(block_size, dtype=bool)

    def finish(block):
        flags = valid[block]
        adjacency = ((self_mask[block] > 0) | identity) & flags[:, None] & flags[None, :]
        scores = jnp.where(adjacency[None], score_block(target_all[block], source_all[block], attn), FLOOR)
        top = jnp.maximum(jnp.maximum(row_peak[block], col_peak[block]), jnp.max(scores, axis=-1))
        weights = jnp.where(adjacency[None], jnp.exp(scores - top[:, :, None]), 0.0)
        own = weigh(weights, source_all[block], heads).reshape(block_size, heads, head_width)
        row_scale = jnp.exp(row_peak[block] - top)
        col_scale = jnp.exp(col_peak[block] - top)
        numer = own + row_numer[block].reshape(block_size, heads, head_width) * row_scale.T[:, :, None]
        numer = numer + col_numer[block].reshape(block_size, heads, head_width) * col_scale.T[:, :, None]
        denom = jnp.sum(weights, axis=-1) + row_denom[block] * row_scale + col_denom[block] * col_scale
        denom = denom + (1.0 - flags.astype(jnp.float32))[None, :]
        result = (numer / denom.T[:, :, None]).reshape(block_size, width) + bias[None, :]
        return result.astype(jnp.bfloat16)

    return lax.map(finish, jnp.arange(blocks, dtype=jnp.int32)).reshape(blocks * block_size, width)
```

```python
import functools

import jax
import jax.numpy as jnp
from jax import lax
from jax.experimental import pallas as pl
from jax.experimental.pallas import tpu as pltpu
from jax.sharding import Mesh, PartitionSpec as P

F32 = jnp.float32
BF16 = jnp.bfloat16
FLOOR = -1e30
BS = 128
HS = 256
EXT = 16
SRC = BS + EXT
ALL = SRC + BS
UNROLL = 64


def split3(value):
    high = value.astype(BF16).astype(F32)
    rest = value - high
    middle = rest.astype(BF16).astype(F32)
    return high, middle, rest - middle


def pack_rows(value):
    high, middle, low = split3(jnp.broadcast_to(value, (EXT, BS)))
    row = lax.broadcasted_iota(jnp.int32, (EXT, BS), 0)
    zero = jnp.zeros_like(high)
    rows = jnp.where(row == 0, high, jnp.where(row == 1, middle, jnp.where(row == 2, low, zero)))
    return jnp.concatenate([rows, zero], axis=1).astype(BF16)


def unpack_rows(rows):
    wide = rows.astype(F32)
    return wide[0:1] + (wide[1:2] + wide[2:3])


def project_kernel(features, valid, attn, weight_src, weight_tgt, out):
    source = jnp.dot(features[...], weight_src[...], preferred_element_type=F32).astype(BF16)
    target = jnp.dot(features[...], weight_tgt[...], preferred_element_type=F32).astype(BF16)
    out[0, :BS, :] = source
    out[0, SRC:, :] = target
    linear = jnp.sum(source.astype(F32) * attn[0], axis=1, keepdims=True)
    linear = jnp.broadcast_to(linear, (BS, BS)).T[0:1]
    out[0, BS:SRC, :] = pack_rows(jnp.where(valid[...] > 0, linear, FLOOR))


def project(features, valid, attn, weight_src, weight_tgt):
    heads = attn.shape[0]
    width = features.shape[1]
    return pl.pallas_call(
        project_kernel,
        grid=(heads,),
        out_shape=jax.ShapeDtypeStruct((heads, ALL, HS), BF16),
        in_specs=[
            pl.BlockSpec((BS, width), lambda h: (0, 0)),
            pl.BlockSpec((1, BS), lambda h: (0, 0)),
            pl.BlockSpec((1, 1, HS), lambda h: (h, 0, 0)),
            pl.BlockSpec((width, HS), lambda h: (0, h)),
            pl.BlockSpec((width, HS), lambda h: (0, h)),
        ],
        out_specs=pl.BlockSpec((1, ALL, HS), lambda h: (h, 0, 0)),
        name="project",
    )(features, valid, attn.reshape(heads, 1, HS), weight_src, weight_tgt)


def score_plane(target, minus, halves):
    lane = lax.broadcasted_iota(jnp.int32, (BS, BS), 1)
    half = BS // 2
    tiled = target.reshape(BS // 16, 16, HS)
    zero = jnp.zeros((BS, BS), F32)

    def step(at, planes):
        planes = list(planes)
        for u in range(UNROLL):
            s = at * UNROLL + u
            chosen = (lane == s) | (lane == s + half)
            for side in range(2):
                row = minus[pl.ds(s + side * half, 1), :]
                row = jnp.broadcast_to(row, (16, HS)).astype(BF16)
                larger = jnp.maximum(tiled, row[None]).reshape(BS, HS)
                sums = jnp.dot(larger, halves, preferred_element_type=F32)
                planes[side] = jnp.where(chosen, sums, planes[side])
        return tuple(planes)

    low, high = lax.fori_loop(0, half // UNROLL, step, (zero, zero))
    low = low + pltpu.roll(low, half, 1)
    high = high + pltpu.roll(high, half, 1)
    return jnp.where(lane < half, low, high)


def attend_kernel(kind, *refs):
    if kind == "self":
        own, masks, halves, out, acc, peak, den, minus = refs
        targets = sources = own
    else:
        count, target_at, source_at, targets, sources, masks, halves, out, acc, peak, den, minus = refs
    blocks = acc.shape[0]

    def clear(b, carry):
        acc[b] = jnp.zeros((BS, HS), F32)
        peak[b] = jnp.full((BS, BS), FLOOR, F32)
        den[b] = jnp.zeros((BS, BS), F32)
        return carry

    lax.fori_loop(0, blocks, clear, 0)

    def one(cell, slot, a, b):
        source = sources[b, :BS, :]
        minus[...] = -source.astype(F32)
        linear = unpack_rows(sources[b, BS:SRC, :BS])
        scores = score_plane(targets[a, SRC:, :], minus, halves[...])
        mask = masks[cell, pl.ds(pl.multiple_of(slot * BS, BS), BS), :].astype(F32)
        if kind == "backward":
            mask = mask.T
        scores = jnp.where(mask > 0, scores + linear, FLOOR)
        before = peak[a]
        top = jnp.maximum(before, jnp.max(scores, axis=1, keepdims=True))
        scale = jnp.exp(before - top)
        weights = jnp.exp(scores - top)
        peak[a] = top
        den[a] = den[a] * scale + jnp.sum(weights, axis=1, keepdims=True)
        acc[a] = acc[a] * jnp.concatenate([scale, scale], axis=1) + jnp.dot(
            weights.astype(BF16), source, preferred_element_type=F32
        )

    if kind == "self":

        def own_step(b, carry):
            one(b, 8, b, b)
            return carry

        lax.fori_loop(0, blocks, own_step, 0)
    else:
        for cell in range(4):

            def step(slot, carry):
                one(cell, slot, target_at[cell * 8 + slot], source_at[cell * 8 + slot])
                return carry

            lax.fori_loop(0, count[cell], step, 0)

    def finish(b, carry):
        total = jnp.maximum(den[b], 1e-30)
        inverse = 1.0 / total
        out[b, :BS, :] = (acc[b] * jnp.concatenate([inverse, inverse], axis=1)).astype(BF16)
        out[b, BS:, :] = pack_rows((peak[b] + jnp.log(total)).T[0:1])
        return carry

    lax.fori_loop(0, blocks, finish, 0)


def attend(kind, blocks, slots, *operands):
    smem = pl.BlockSpec(memory_space=pltpu.SMEM)
    vmem = pl.BlockSpec(memory_space=pltpu.VMEM)
    scalars = 0 if kind == "self" else 3
    return pl.pallas_call(
        functools.partial(attend_kernel, kind),
        out_shape=jax.ShapeDtypeStruct((blocks, SRC, HS), BF16),
        in_specs=[smem] * scalars + [vmem] * (len(operands) - scalars),
        out_specs=vmem,
        scratch_shapes=[
            pltpu.VMEM((blocks, BS, HS), F32),
            pltpu.VMEM((blocks, BS, BS), F32),
            pltpu.VMEM((blocks, BS, BS), F32),
            pltpu.VMEM((BS, HS), F32),
        ],
        compiler_params=pltpu.CompilerParams(vmem_limit_bytes=40 << 20),
        cost_estimate=pl.CostEstimate(
            flops=slots * BS * BS * HS * 256, bytes_accessed=1 << 20, transcendentals=0
        ),
        name="attend_" + kind,
    )(*operands)


def merge_kernel(rows, cols, own, bias, out):
    parts = [rows.at[p, 0] for p in range(8)] + [cols.at[p, 0] for p in range(8)] + [own.at[0]]
    sums = [unpack_rows(part[BS:SRC, :BS]) for part in parts]
    top = functools.reduce(jnp.maximum, sums)
    shares = [jnp.exp(value - top) for value in sums]
    total = functools.reduce(jnp.add, shares)
    table = jnp.concatenate([share / total for share in shares] + [jnp.zeros((BS - 17, BS), F32)])
    table = table.T
    result = jnp.zeros((BS, HS), F32)
    for p, part in enumerate(parts):
        result = result + part[:BS, :].astype(F32) * table[:, p : p + 1]
    out[0] = (result + bias[...]).astype(BF16)


def merge(rows, cols, own, bias):
    blocks = own.shape[0]
    return pl.pallas_call(
        merge_kernel,
        grid=(blocks,),
        out_shape=jax.ShapeDtypeStruct((blocks, BS, HS), BF16),
        in_specs=[
            pl.BlockSpec((8, 1, SRC, HS), lambda b: (0, b, 0, 0)),
            pl.BlockSpec((8, 1, SRC, HS), lambda b: (0, b, 0, 0)),
            pl.BlockSpec((1, SRC, HS), lambda b: (b, 0, 0)),
            pl.BlockSpec((1, HS), lambda b: (0, 0)),
        ],
        out_specs=pl.BlockSpec((1, BS, HS), lambda b: (b, 0, 0)),
        name="merge",
    )(rows, cols, own, bias)


def body(
    features,
    node_valid,
    self_mask,
    pair_blocks,
    pair_count,
    pair_masks,
    weight_src,
    weight_tgt,
    attn,
    bias,
):
    heads = attn.shape[0]
    group = ("rp", "cp")
    row_part, col_part = lax.axis_index("rp"), lax.axis_index("cp")
    head = row_part * 2 + col_part

    identity = jnp.eye(BS, dtype=bool)
    own_mask = (self_mask[0] > 0) | identity
    first, second = pair_blocks[0, 0, :, 0] % 16, pair_blocks[0, 0, :, 1] // 16
    first_at = (first // 2) * 4 + row_part * 2 + first % 2
    second_at = (second // 2) * 4 + (second % 2) * 2 + col_part
    info = jnp.stack([first_at, second_at, jnp.broadcast_to(pair_count[0, 0], (8,))])
    info = jnp.pad(info, ((0, EXT - 3), (0, BS - 8)))
    cell = jnp.concatenate(
        [
            pair_masks.reshape(8 * BS, BS).astype(BF16),
            own_mask.astype(BF16),
            info.astype(BF16),
        ]
    )
    cells = lax.all_gather(cell[None], group, axis=0, tiled=True)
    lists = cells[:, 9 * BS : 9 * BS + 3, :8].astype(jnp.int32)
    first_at, second_at = lists[:, 0].reshape(32), lists[:, 1].reshape(32)
    count = lists[:, 2, 0]

    own_heads = project(features, node_valid, attn, weight_src, weight_tgt)
    mine = lax.all_to_all(own_heads, group, 0, 0, tiled=True)
    row_side = lax.all_gather(mine, "C", axis=0, tiled=True)
    col_side = lax.all_gather(mine, "R", axis=0, tiled=True)

    scaled = 0.8 * lax.dynamic_index_in_dim(attn, head, 0, keepdims=False)
    high = lax.reduce_precision(scaled, 8, 7)
    low = scaled - high
    halves = jnp.concatenate(
        [jnp.broadcast_to(part[:, None], (HS, BS // 2)) for part in (high, low)], axis=1
    ).astype(BF16)

    own = attend("self", 4, 4, mine, cells, halves)
    to_rows = attend(
        "forward", 32, 16, count, first_at, second_at, row_side, col_side, cells, halves
    )
    to_cols = attend(
        "backward", 32, 16, count, second_at, first_at, col_side, row_side, cells, halves
    )
    rows = lax.all_to_all(to_rows, "C", 0, 0, tiled=True).reshape(8, 4, SRC, HS)
    cols = lax.all_to_all(to_cols, "R", 0, 0, tiled=True).reshape(8, 4, SRC, HS)
    bias_head = lax.dynamic_index_in_dim(bias.reshape(heads, HS), head, 0)
    merged = merge(rows, cols, own, bias_head)
    merged = lax.all_to_all(merged, group, 0, 0, tiled=True)
    result = merged.transpose(1, 0, 2).reshape(BS, heads * HS)
    return jnp.where(node_valid[0][:, None] > 0, result, bias.astype(BF16)[None, :])


def solution(mesh):
    fine = Mesh(mesh.devices.reshape(8, 2, 8, 2), ("R", "rp", "C", "cp"))
    row, col = ("R", "rp"), ("C", "cp")
    both = row + col
    return jax.shard_map(
        body,
        mesh=fine,
        in_specs=(
            P(both, None),
            P(both, None),
            P(both, None, None),
            P(row, col, None, None),
            P(row, col),
            P(row, col, None, None, None),
            P(),
            P(),
            P(),
            P(),
        ),
        out_specs=P(both, None),
        check_vma=False,
    )
```

```python
import functools

import jax
import jax.numpy as jnp
from jax import lax
from jax.experimental import pallas as pl
from jax.experimental.pallas import tpu as pltpu
from jax.sharding import Mesh, PartitionSpec as P

F32 = jnp.float32
BF16 = jnp.bfloat16
FLOOR = -1e30
BS = 128
HS = 256
EXT = 16
SRC = BS + EXT
ALL = SRC + BS
UNROLL = 64


def split3(value):
    high = value.astype(BF16).astype(F32)
    rest = value - high
    middle = rest.astype(BF16).astype(F32)
    return high, middle, rest - middle


def pack_rows(value):
    high, middle, low = split3(jnp.broadcast_to(value, (EXT, BS)))
    row = lax.broadcasted_iota(jnp.int32, (EXT, BS), 0)
    zero = jnp.zeros_like(high)
    rows = jnp.where(row == 0, high, jnp.where(row == 1, middle, jnp.where(row == 2, low, zero)))
    return jnp.concatenate([rows, zero], axis=1).astype(BF16)


def unpack_rows(rows):
    wide = rows.astype(F32)
    return wide[0:1] + (wide[1:2] + wide[2:3])


def project_kernel(features, valid, attn, weight_src, weight_tgt, out):
    source = jnp.dot(features[...], weight_src[...], preferred_element_type=F32).astype(BF16)
    target = jnp.dot(features[...], weight_tgt[...], preferred_element_type=F32).astype(BF16)
    out[0, :BS, :] = source
    out[0, SRC:, :] = target
    linear = jnp.sum(source.astype(F32) * attn[0], axis=1, keepdims=True)
    linear = jnp.broadcast_to(linear, (BS, BS)).T[0:1]
    out[0, BS:SRC, :] = pack_rows(jnp.where(valid[...] > 0, linear, FLOOR))


def project(features, valid, attn, weight_src, weight_tgt):
    heads = attn.shape[0]
    width = features.shape[1]
    return pl.pallas_call(
        project_kernel,
        grid=(heads,),
        out_shape=jax.ShapeDtypeStruct((heads, ALL, HS), BF16),
        in_specs=[
            pl.BlockSpec((BS, width), lambda h: (0, 0)),
            pl.BlockSpec((1, BS), lambda h: (0, 0)),
            pl.BlockSpec((1, 1, HS), lambda h: (h, 0, 0)),
            pl.BlockSpec((width, HS), lambda h: (0, h)),
            pl.BlockSpec((width, HS), lambda h: (0, h)),
        ],
        out_specs=pl.BlockSpec((1, ALL, HS), lambda h: (h, 0, 0)),
        name="project",
    )(features, valid, attn.reshape(heads, 1, HS), weight_src, weight_tgt)


def score_plane(target, minus, halves):
    lane = lax.broadcasted_iota(jnp.int32, (BS, BS), 1)
    half = BS // 2
    tiled = target.reshape(BS // 16, 16, HS)
    zero = jnp.zeros((BS, BS), F32)

    def step(at, planes):
        planes = list(planes)
        for u in range(UNROLL):
            s = at * UNROLL + u
            chosen = (lane == s) | (lane == s + half)
            for side in range(2):
                row = minus[pl.ds(s + side * half, 1), :]
                row = jnp.broadcast_to(row, (16, HS)).astype(BF16)
                larger = jnp.maximum(tiled, row[None]).reshape(BS, HS)
                sums = jnp.dot(larger, halves, preferred_element_type=F32)
                planes[side] = jnp.where(chosen, sums, planes[side])
        return tuple(planes)

    low, high = lax.fori_loop(0, half // UNROLL, step, (zero, zero))
    low = low + pltpu.roll(low, half, 1)
    high = high + pltpu.roll(high, half, 1)
    return jnp.where(lane < half, low, high)


def attend_kernel(kind, split, *refs):
    if kind == "self":
        target_pieces, source_pieces, (masks, halves, out, acc, peak, den, minus) = refs[:1], refs[1:2], refs[2:]
        targets, sources = target_pieces[0], source_pieces[0]
    else:
        count, target_at, source_at, out_at, masks, halves = refs[:6]
        target_pieces, source_pieces = refs[6 : 6 + split[0]], refs[6 + split[0] : 6 + sum(split)]
        out, acc, peak, den, minus, targets, sources, sems = refs[6 + sum(split) :]
    blocks = acc.shape[0]
    copies = []
    if kind != "self":
        for pieces, table in ((target_pieces, targets), (source_pieces, sources)):
            at = 0
            for piece in pieces:
                size = piece.shape[0]
                copies.append(
                    pltpu.make_async_copy(piece, table.at[pl.ds(at, size)], sems.at[len(copies)])
                )
                at += size
    for copy in copies:
        copy.start()

    def clear(b, carry):
        acc[b] = jnp.zeros((BS, HS), F32)
        peak[b] = jnp.full((BS, BS), FLOOR, F32)
        den[b] = jnp.zeros((BS, BS), F32)
        return carry

    lax.fori_loop(0, blocks, clear, 0)
    for copy in copies:
        copy.wait()

    def one(cell, slot, a, b, c):
        source = sources[b, :BS, :]
        minus[...] = -source.astype(F32)
        linear = unpack_rows(sources[b, BS:SRC, :BS])
        scores = score_plane(targets[a], minus, halves[...])
        mask = masks[cell, pl.ds(pl.multiple_of(slot * BS, BS), BS), :].astype(F32)
        if kind == "backward":
            mask = mask.T
        scores = jnp.where(mask > 0, scores + linear, FLOOR)
        before = peak[c]
        top = jnp.maximum(before, jnp.max(scores, axis=1, keepdims=True))
        scale = jnp.exp(before - top)
        weights = jnp.exp(scores - top)
        peak[c] = top
        den[c] = den[c] * scale + jnp.sum(weights, axis=1, keepdims=True)
        acc[c] = acc[c] * jnp.concatenate([scale, scale], axis=1) + jnp.dot(
            weights.astype(BF16), source, preferred_element_type=F32
        )

    if kind == "self":

        def own_step(b, carry):
            one(b, 8, b, b, b)
            return carry

        lax.fori_loop(0, blocks, own_step, 0)
    else:
        for cell in range(4):

            def step(slot, carry):
                at = cell * 8 + slot
                one(cell, slot, target_at[at], source_at[at], out_at[at])
                return carry

            lax.fori_loop(0, count[cell], step, 0)

    def finish(b, carry):
        total = jnp.maximum(den[b], 1e-30)
        inverse = 1.0 / total
        out[b, :BS, :] = (acc[b] * jnp.concatenate([inverse, inverse], axis=1)).astype(BF16)
        out[b, BS:, :] = pack_rows((peak[b] + jnp.log(total)).T[0:1])
        return carry

    lax.fori_loop(0, blocks, finish, 0)


def attend(kind, lists, masks, halves, targets, sources):
    smem = pl.BlockSpec(memory_space=pltpu.SMEM)
    vmem = pl.BlockSpec(memory_space=pltpu.VMEM)
    hbm = pl.BlockSpec(memory_space=pltpu.HBM)
    split = (len(targets), len(sources))
    blocks = 4 if kind == "self" else 32
    slots = 4 if kind == "self" else 16
    scratch = [
        pltpu.VMEM((blocks, BS, HS), F32),
        pltpu.VMEM((blocks, BS, BS), F32),
        pltpu.VMEM((blocks, BS, BS), F32),
        pltpu.VMEM((BS, HS), F32),
    ]
    if kind == "self":
        operands = (*targets, *sources, masks, halves)
        specs = [vmem] * 4
    else:
        operands = (*lists, masks, halves, *targets, *sources)
        specs = [smem] * 4 + [vmem] * 2 + [hbm] * sum(split)
        scratch += [
            pltpu.VMEM((blocks, BS, HS), BF16),
            pltpu.VMEM((blocks, SRC, HS), BF16),
            pltpu.SemaphoreType.DMA((sum(split),)),
        ]
    return pl.pallas_call(
        functools.partial(attend_kernel, kind, split),
        out_shape=jax.ShapeDtypeStruct((blocks, SRC, HS), BF16),
        in_specs=specs,
        out_specs=vmem,
        scratch_shapes=scratch,
        compiler_params=pltpu.CompilerParams(vmem_limit_bytes=(16 if kind == "self" else 56) << 20),
        cost_estimate=pl.CostEstimate(
            flops=slots * BS * BS * HS * 512, bytes_accessed=1 << 20, transcendentals=0
        ),
        name="attend_" + kind,
    )(*operands)


def merge_kernel(rows, cols, own, bias, out):
    parts = [rows.at[p, 0] for p in range(8)] + [cols.at[p, 0] for p in range(8)] + [own.at[0]]
    sums = [unpack_rows(part[BS:SRC, :BS]) for part in parts]
    top = functools.reduce(jnp.maximum, sums)
    shares = [jnp.exp(value - top) for value in sums]
    total = functools.reduce(jnp.add, shares)
    table = jnp.concatenate([share / total for share in shares] + [jnp.zeros((BS - 17, BS), F32)])
    table = table.T
    result = jnp.zeros((BS, HS), F32)
    for p, part in enumerate(parts):
        result = result + part[:BS, :].astype(F32) * table[:, p : p + 1]
    out[0] = (result + bias[...]).astype(BF16)


def merge(rows, cols, own, bias):
    blocks = own.shape[0]
    return pl.pallas_call(
        merge_kernel,
        grid=(blocks,),
        out_shape=jax.ShapeDtypeStruct((blocks, BS, HS), BF16),
        in_specs=[
            pl.BlockSpec((8, 1, SRC, HS), lambda b: (0, b, 0, 0)),
            pl.BlockSpec((8, 1, SRC, HS), lambda b: (0, b, 0, 0)),
            pl.BlockSpec((1, SRC, HS), lambda b: (b, 0, 0)),
            pl.BlockSpec((1, HS), lambda b: (0, 0)),
        ],
        out_specs=pl.BlockSpec((1, BS, HS), lambda b: (b, 0, 0)),
        name="merge",
    )(rows, cols, own, bias)


def body(
    features,
    node_valid,
    self_mask,
    pair_blocks,
    pair_count,
    pair_masks,
    weight_src,
    weight_tgt,
    attn,
    bias,
):
    heads = attn.shape[0]
    group = ("rp", "cp")
    row_part, col_part = lax.axis_index("rp"), lax.axis_index("cp")
    head = row_part * 2 + col_part

    identity = jnp.eye(BS, dtype=bool)
    own_mask = (self_mask[0] > 0) | identity
    first, second = pair_blocks[0, 0, :, 0] % 16, pair_blocks[0, 0, :, 1] // 16
    first_at = (first // 2) * 4 + row_part * 2 + first % 2
    second_at = (second // 2) * 4 + (second % 2) * 2 + col_part
    info = jnp.stack([first_at, second_at, jnp.broadcast_to(pair_count[0, 0], (8,))])
    info = jnp.pad(info, ((0, EXT - 3), (0, BS - 8)))
    cell = jnp.concatenate(
        [
            pair_masks.reshape(8 * BS, BS).astype(BF16),
            own_mask.astype(BF16),
            info.astype(BF16),
        ]
    )
    cells = lax.all_gather(cell[None], group, axis=0, tiled=True)
    lists = cells[:, 9 * BS : 9 * BS + 3, :8].astype(jnp.int32)
    first_at, second_at = lists[:, 0].reshape(32), lists[:, 1].reshape(32)
    count = lists[:, 2, 0]
    me = lax.axis_index("R")
    from_row = second_at // 4
    y_steps = (me // 2 - from_row // 2) % 4
    x_steps = (me + from_row) % 2
    second_near = (y_steps * 2 + x_steps) * 4 + second_at % 4

    own_heads = project(features, node_valid, attn, weight_src, weight_tgt)
    mine = lax.all_to_all(own_heads, group, 0, 0, tiled=True)
    source, target = mine[:, :SRC], mine[:, SRC:]

    size = lax.axis_size("R")
    across = [(i, i ^ 1) for i in range(size)]
    around = [[(i, (i + 2 * k) % size) for i in range(size)] for k in (1, 2, 3)]
    row_targets = lax.all_gather(target, "C", axis=0, tiled=True)
    source_beside = lax.ppermute(source, "R", across)
    target_beside = lax.ppermute(target, "R", across)
    col_sources = [source, source_beside]
    for way in around:
        col_sources += [lax.ppermute(source, "R", way), lax.ppermute(source_beside, "R", way)]

    scaled = 0.8 * lax.dynamic_index_in_dim(attn, head, 0, keepdims=False)
    high = lax.reduce_precision(scaled, 8, 7)
    low = scaled - high
    halves = jnp.concatenate(
        [jnp.broadcast_to(part[:, None], (HS, BS // 2)) for part in (high, low)], axis=1
    ).astype(BF16)

    own = attend("self", (), cells, halves, [target], [source])
    both = jnp.concatenate([target, target_beside])
    (row_targets, *col_sources), both, later_source, own = lax.optimization_barrier(
        ((row_targets, *col_sources), both, source, own)
    )
    row_sources = lax.all_gather(later_source, "C", axis=0, tiled=True)
    col_targets = [both] + [lax.ppermute(both, "R", way) for way in around]
    to_rows = attend(
        "forward", (count, first_at, second_near, first_at), cells, halves, [row_targets], col_sources
    )
    to_rows, col_targets = lax.optimization_barrier((to_rows, col_targets))
    to_cols = attend(
        "backward", (count, second_near, first_at, second_at), cells, halves, col_targets, [row_sources]
    )
    rows = lax.all_to_all(to_rows, "C", 0, 0, tiled=True).reshape(8, 4, SRC, HS)
    cols = lax.all_to_all(to_cols, "R", 0, 0, tiled=True).reshape(8, 4, SRC, HS)
    bias_head = lax.dynamic_index_in_dim(bias.reshape(heads, HS), head, 0)
    merged = merge(rows, cols, own, bias_head)
    merged = lax.all_to_all(merged, group, 0, 0, tiled=True)
    result = merged.transpose(1, 0, 2).reshape(BS, heads * HS)
    return jnp.where(node_valid[0][:, None] > 0, result, bias.astype(BF16)[None, :])


def solution(mesh):
    fine = Mesh(mesh.devices.reshape(8, 2, 8, 2), ("R", "rp", "C", "cp"))
    row, col = ("R", "rp"), ("C", "cp")
    both = row + col
    return jax.shard_map(
        body,
        mesh=fine,
        in_specs=(
            P(both, None),
            P(both, None),
            P(both, None, None),
            P(row, col, None, None),
            P(row, col),
            P(row, col, None, None, None),
            P(),
            P(),
            P(),
            P(),
        ),
        out_specs=P(both, None),
        check_vma=False,
    )
```

```python
import functools

import jax
import jax.numpy as jnp
from jax import lax
from jax.experimental import pallas as pl
from jax.experimental.pallas import tpu as pltpu
from jax.sharding import Mesh, PartitionSpec as P

F32 = jnp.float32
BF16 = jnp.bfloat16
FLOOR = -1e30
BS = 128
HS = 256
EXT = 16
SRC = BS + EXT
ALL = SRC + BS
PER_DOT = 4


def split3(value):
    high = value.astype(BF16).astype(F32)
    rest = value - high
    middle = rest.astype(BF16).astype(F32)
    return high, middle, rest - middle


def pack_rows(value):
    high, middle, low = split3(jnp.broadcast_to(value, (EXT, BS)))
    row = lax.broadcasted_iota(jnp.int32, (EXT, BS), 0)
    zero = jnp.zeros_like(high)
    rows = jnp.where(row == 0, high, jnp.where(row == 1, middle, jnp.where(row == 2, low, zero)))
    return jnp.concatenate([rows, zero], axis=1).astype(BF16)


def unpack_rows(rows):
    wide = rows.astype(F32)
    return wide[0:1] + (wide[1:2] + wide[2:3])


def project_kernel(place, features, valid, attn, weight_src, weight_tgt, *outs):
    step = pl.program_id(0)
    source = jnp.dot(features[...], weight_src[...], preferred_element_type=F32).astype(BF16)
    target = jnp.dot(features[...], weight_tgt[...], preferred_element_type=F32).astype(BF16)
    linear = jnp.sum(
        source.astype(F32) * attn[pl.ds(step ^ place[0], 1), :], axis=1, keepdims=True
    )
    linear = jnp.broadcast_to(linear, (BS, BS)).T[0:1]
    extra = pack_rows(jnp.where(valid[...] > 0, linear, FLOOR))
    for d, out in enumerate(outs):

        @pl.when(step == d)
        def _():
            out[:BS, :] = source
            out[BS:SRC, :] = extra
            out[SRC:, :] = target


def project(place, features, valid, attn, weight_src, weight_tgt):
    heads = attn.shape[0]
    width = features.shape[1]
    return pl.pallas_call(
        project_kernel,
        grid_spec=pltpu.PrefetchScalarGridSpec(
            num_scalar_prefetch=1,
            grid=(heads,),
            in_specs=[
                pl.BlockSpec((BS, width), lambda d, place: (0, 0)),
                pl.BlockSpec((1, BS), lambda d, place: (0, 0)),
                pl.BlockSpec((heads, HS), lambda d, place: (0, 0)),
                pl.BlockSpec((width, HS), lambda d, place: (0, d ^ place[0])),
                pl.BlockSpec((width, HS), lambda d, place: (0, d ^ place[0])),
            ],
            out_specs=[pl.BlockSpec((ALL, HS), lambda d, place: (0, 0))] * heads,
        ),
        out_shape=[jax.ShapeDtypeStruct((ALL, HS), BF16)] * heads,
        name="project",
    )(place, features, valid, attn, weight_src, weight_tgt)


def gather_kernel(*refs):
    parts, (source, target) = refs[:4], refs[4:]
    for d, part in enumerate(parts):
        source[d] = part[:SRC, :]
        target[d] = part[SRC:, :]


def gather_square(parts):
    return pl.pallas_call(
        gather_kernel,
        out_shape=[
            jax.ShapeDtypeStruct((4, SRC, HS), BF16),
            jax.ShapeDtypeStruct((4, BS, HS), BF16),
        ],
        name="gather_square",
    )(*parts)


def pair_kernel(first, second, out):
    out[:4] = first[...]
    out[4:] = second[...]


def pair(first, second):
    return pl.pallas_call(
        pair_kernel, out_shape=jax.ShapeDtypeStruct((8, *first.shape[1:]), BF16), name="pair"
    )(first, second)


def score_plane(target, minus, wide, halves, scaled, planes):
    lane = lax.broadcasted_iota(jnp.int32, (BS, BS), 1)
    half = BS // 2
    wide[...] = target.astype(F32)
    tiled = wide[...].astype(BF16).reshape(BS // 16, 16, HS)
    weights = halves[...]
    left, right = scaled[:, :BS], scaled[:, BS:]
    waiting = []

    def flush():
        tiles = []
        for u, side in waiting:
            row = minus[u + side * half : u + side * half + 1, :]
            row = jnp.broadcast_to(row, (16, HS)).astype(BF16)
            tiles.append(jnp.maximum(tiled, row[None]).reshape(BS, HS))
        sums = jnp.dot(jnp.concatenate(tiles), weights, preferred_element_type=F32)
        for at, (u, side) in enumerate(waiting):
            pltpu.store(
                planes.at[side], sums[at * BS : (at + 1) * BS], mask=(lane == u) | (lane == u + half)
            )
        waiting.clear()

    for u in range(half):
        for side in range(2):
            if u % 2 == 0:
                waiting.append((u, side))
                if len(waiting) == PER_DOT:
                    flush()
            else:
                s = u + side * half
                row = minus[s : s + 1, :]
                terms = (
                    jnp.maximum(wide[:, :BS], row[:, :BS]) * left
                    + jnp.maximum(wide[:, BS:], row[:, BS:]) * right
                )
                sums = jnp.broadcast_to(jnp.sum(terms, axis=1, keepdims=True), (BS, BS))
                pltpu.store(planes.at[2], sums, mask=lane == s)
    low, high = planes[0], planes[1]
    low = low + pltpu.roll(low, half, 1)
    high = high + pltpu.roll(high, half, 1)
    return jnp.where(lane % 2 == 1, planes[2], jnp.where(lane < half, low, high))


def attend_kernel(kind, split, *refs):
    if kind == "self":
        target_pieces, source_pieces, (masks, halves, scaled, out, acc, peak, den, minus, wide, planes) = refs[:1], refs[1:2], refs[2:]
        targets, sources = target_pieces[0], source_pieces[0]
    else:
        count, target_at, source_at, out_at, masks, halves, scaled = refs[:7]
        target_pieces, source_pieces = refs[7 : 7 + split[0]], refs[7 + split[0] : 7 + sum(split)]
        out, acc, peak, den, minus, wide, planes, targets, sources, sems = refs[7 + sum(split) :]
    blocks = acc.shape[0]
    copies = []
    if kind != "self":
        for pieces, table in ((target_pieces, targets), (source_pieces, sources)):
            at = 0
            for piece in pieces:
                size = piece.shape[0]
                copies.append(
                    pltpu.make_async_copy(piece, table.at[pl.ds(at, size)], sems.at[len(copies)])
                )
                at += size
    for copy in copies:
        copy.start()

    def clear(b, carry):
        acc[b] = jnp.zeros((BS, HS), F32)
        peak[b] = jnp.full((BS, BS), FLOOR, F32)
        den[b] = jnp.zeros((BS, BS), F32)
        return carry

    lax.fori_loop(0, blocks, clear, 0)
    for copy in copies:
        copy.wait()

    def one(cell, slot, a, b, c):
        source = sources[b, :BS, :]
        minus[...] = -source.astype(F32)
        linear = unpack_rows(sources[b, BS:SRC, :BS])
        scores = score_plane(targets[a], minus, wide, halves, scaled[...], planes)
        mask = masks[cell, pl.ds(pl.multiple_of(slot * BS, BS), BS), :].astype(F32)
        if kind == "backward":
            mask = mask.T
        scores = jnp.where(mask > 0, scores + linear, FLOOR)
        before = peak[c]
        top = jnp.maximum(before, jnp.max(scores, axis=1, keepdims=True))
        scale = jnp.exp(before - top)
        weights = jnp.exp(scores - top)
        peak[c] = top
        den[c] = den[c] * scale + jnp.sum(weights, axis=1, keepdims=True)
        acc[c] = acc[c] * jnp.concatenate([scale, scale], axis=1) + jnp.dot(
            weights.astype(BF16), source, preferred_element_type=F32
        )

    if kind == "self":

        def own_step(b, carry):
            one(b, 8, b, b, b)
            return carry

        lax.fori_loop(0, blocks, own_step, 0)
    else:
        ends = [count[0], count[0] + count[1], count[0] + count[1] + count[2]]

        def step(i, carry):
            cell, start = jnp.int32(0), jnp.int32(0)
            for end in ends:
                past = i >= end
                cell = cell + jnp.where(past, 1, 0)
                start = jnp.where(past, end, start)
            slot = i - start
            at = cell * 8 + slot
            one(cell, slot, target_at[at], source_at[at], out_at[at])
            return carry

        lax.fori_loop(0, ends[2] + count[3], step, 0)

    def finish(b, carry):
        total = jnp.maximum(den[b], 1e-30)
        inverse = 1.0 / total
        out[b, :BS, :] = (acc[b] * jnp.concatenate([inverse, inverse], axis=1)).astype(BF16)
        out[b, BS:, :] = pack_rows((peak[b] + jnp.log(total)).T[0:1])
        return carry

    lax.fori_loop(0, blocks, finish, 0)


def attend(kind, lists, masks, attn, targets, sources):
    smem = pl.BlockSpec(memory_space=pltpu.SMEM)
    vmem = pl.BlockSpec(memory_space=pltpu.VMEM)
    hbm = pl.BlockSpec(memory_space=pltpu.HBM)
    split = (len(targets), len(sources))
    blocks = 4 if kind == "self" else 32
    slots = 4 if kind == "self" else 16
    scratch = [
        pltpu.VMEM((blocks, BS, HS), F32),
        pltpu.VMEM((blocks, BS, BS), F32),
        pltpu.VMEM((blocks, BS, BS), F32),
        pltpu.VMEM((BS, HS), F32),
        pltpu.VMEM((BS, HS), F32),
        pltpu.VMEM((3, BS, BS), F32),
    ]
    if kind == "self":
        operands = (*targets, *sources, masks, *attn)
        specs = [vmem] * 5
    else:
        operands = (*lists, masks, *attn, *targets, *sources)
        specs = [smem] * 4 + [vmem] * 3 + [hbm] * sum(split)
        scratch += [
            pltpu.VMEM((blocks, BS, HS), BF16),
            pltpu.VMEM((blocks, SRC, HS), BF16),
            pltpu.SemaphoreType.DMA((sum(split),)),
        ]
    return pl.pallas_call(
        functools.partial(attend_kernel, kind, split),
        out_shape=jax.ShapeDtypeStruct((blocks, SRC, HS), BF16),
        in_specs=specs,
        out_specs=vmem,
        scratch_shapes=scratch,
        compiler_params=pltpu.CompilerParams(vmem_limit_bytes=(16 if kind == "self" else 56) << 20),
        cost_estimate=pl.CostEstimate(
            flops=slots * BS * BS * HS * 512, bytes_accessed=1 << 20, transcendentals=0
        ),
        name="attend_" + kind,
    )(*operands)


def merge_kernel(place, rows, cols, own, bias, out):
    parts = [rows.at[p, 0] for p in range(8)] + [cols.at[p, 0] for p in range(8)] + [own.at[0]]
    sums = [unpack_rows(part[BS:SRC, :BS]) for part in parts]
    top = functools.reduce(jnp.maximum, sums)
    shares = [jnp.exp(value - top) for value in sums]
    total = functools.reduce(jnp.add, shares)
    table = jnp.concatenate([share / total for share in shares] + [jnp.zeros((BS - 17, BS), F32)])
    table = table.T
    result = jnp.zeros((BS, HS), F32)
    for p, part in enumerate(parts):
        result = result + part[:BS, :].astype(F32) * table[:, p : p + 1]
    out[0] = (result + bias[...]).astype(BF16)


def merge(place, rows, cols, own, bias):
    blocks = own.shape[0]
    return pl.pallas_call(
        merge_kernel,
        grid_spec=pltpu.PrefetchScalarGridSpec(
            num_scalar_prefetch=1,
            grid=(blocks,),
            in_specs=[
                pl.BlockSpec((8, 1, SRC, HS), lambda d, place: (0, d, 0, 0)),
                pl.BlockSpec((8, 1, SRC, HS), lambda d, place: (0, d, 0, 0)),
                pl.BlockSpec((1, SRC, HS), lambda d, place: (d, 0, 0)),
                pl.BlockSpec((1, HS), lambda d, place: (0, 0)),
            ],
            out_specs=pl.BlockSpec((1, BS, HS), lambda d, place: (d ^ place[0], 0, 0)),
        ),
        out_shape=jax.ShapeDtypeStruct((blocks, BS, HS), BF16),
        name="merge",
    )(place, rows, cols, own, bias)


def body(
    features,
    node_valid,
    self_mask,
    pair_blocks,
    pair_count,
    pair_masks,
    weight_src,
    weight_tgt,
    attn,
    bias,
):
    heads = attn.shape[0]
    group = ("rp", "cp")
    row_part, col_part = lax.axis_index("rp"), lax.axis_index("cp")
    head = row_part * 2 + col_part

    place = head.reshape(1)

    def swap(d, value):
        return lax.ppermute(value, group, [(i, i ^ d) for i in range(4)])

    sent = project(place, features, node_valid, attn, weight_src, weight_tgt)
    sent, pair_masks = lax.optimization_barrier((sent, pair_masks))
    mine = [sent[0]] + [swap(d, sent[d]) for d in (1, 2, 3)]

    identity = jnp.eye(BS, dtype=bool)
    own_mask = (self_mask[0] > 0) | identity
    first, second = pair_blocks[0, 0, :, 0] % 16, pair_blocks[0, 0, :, 1] // 16
    first_at = (first // 2) * 4 + row_part * 2 + first % 2
    second_at = (second // 2) * 4 + (second % 2) * 2 + col_part
    info = jnp.stack([first_at, second_at, jnp.broadcast_to(pair_count[0, 0], (8,))])
    info = jnp.pad(info, ((0, EXT - 3), (0, BS - 8)))
    cell = jnp.concatenate(
        [
            pair_masks.reshape(8 * BS, BS).astype(BF16),
            own_mask.astype(BF16),
            info.astype(BF16),
        ]
    )
    cells = jnp.stack([cell] + [swap(d, cell) for d in (1, 2, 3)])
    lists = cells[:, 9 * BS : 9 * BS + 3, :8].astype(jnp.int32)
    first_at, second_at = lists[:, 0].reshape(32) ^ head, lists[:, 1].reshape(32) ^ head
    count = lists[:, 2, 0]
    me = lax.axis_index("R")
    from_row = second_at // 4
    y_steps = (me // 2 - from_row // 2) % 4
    x_steps = (me + from_row) % 2
    second_near = (y_steps * 2 + x_steps) * 4 + second_at % 4

    source, target = gather_square(mine)

    size = lax.axis_size("R")
    across = [(i, i ^ 1) for i in range(size)]
    around = [[(i, (i + 2 * k) % size) for i in range(size)] for k in (1, 2, 3)]
    row_targets = lax.all_gather(target, "C", axis=0, tiled=True)
    source_beside = lax.ppermute(source, "R", across)
    target_beside = lax.ppermute(target, "R", across)
    col_sources = [source, source_beside]
    for way in around:
        col_sources += [lax.ppermute(source, "R", way), lax.ppermute(source_beside, "R", way)]

    scaled = 0.8 * lax.dynamic_index_in_dim(attn, head, 0, keepdims=False)
    high = lax.reduce_precision(scaled, 8, 7)
    low = scaled - high
    halves = jnp.concatenate(
        [jnp.broadcast_to(part[:, None], (HS, BS // 2)) for part in (high, low)], axis=1
    ).astype(BF16)
    shared = (halves, scaled[None])

    own = attend("self", (), cells, shared, [target], [source])
    both = pair(target, target_beside)
    (row_targets, *col_sources), both, later_source, own = lax.optimization_barrier(
        ((row_targets, *col_sources), both, source, own)
    )
    row_sources = lax.all_gather(later_source, "C", axis=0, tiled=True)
    col_targets = [both] + [lax.ppermute(both, "R", way) for way in around]
    to_rows = attend(
        "forward", (count, first_at, second_near, first_at), cells, shared, [row_targets], col_sources
    )
    to_rows, col_targets = lax.optimization_barrier((to_rows, col_targets))
    to_cols = attend(
        "backward", (count, second_near, first_at, second_at), cells, shared, col_targets, [row_sources]
    )
    rows = lax.all_to_all(to_rows, "C", 0, 0, tiled=True).reshape(8, 4, SRC, HS)
    cols = lax.all_to_all(to_cols, "R", 0, 0, tiled=True).reshape(8, 4, SRC, HS)
    bias_head = lax.dynamic_index_in_dim(bias.reshape(heads, HS), head, 0)
    merged = merge(place, rows, cols, own, bias_head)
    merged = lax.all_to_all(merged, group, 0, 0, tiled=True)
    result = merged.transpose(1, 0, 2).reshape(BS, heads * HS)
    return jnp.where(node_valid[0][:, None] > 0, result, bias.astype(BF16)[None, :])


def solution(mesh):
    fine = Mesh(mesh.devices.reshape(8, 2, 8, 2), ("R", "rp", "C", "cp"))
    row, col = ("R", "rp"), ("C", "cp")
    both = row + col
    return jax.shard_map(
        body,
        mesh=fine,
        in_specs=(
            P(both, None),
            P(both, None),
            P(both, None, None),
            P(row, col, None, None),
            P(row, col),
            P(row, col, None, None, None),
            P(),
            P(),
            P(),
            P(),
        ),
        out_specs=P(both, None),
        check_vma=False,
    )
```

```python
import functools

import jax
import jax.numpy as jnp
from jax import lax
from jax.experimental import pallas as pl
from jax.experimental.pallas import tpu as pltpu
from jax.sharding import Mesh, PartitionSpec as P

F32 = jnp.float32
BF16 = jnp.bfloat16
FLOOR = -1e30
BS = 128
HS = 256
EXT = 16
SRC = BS + EXT
ALL = SRC + BS
PER_DOT = 4


def split3(value):
    high = value.astype(BF16).astype(F32)
    rest = value - high
    middle = rest.astype(BF16).astype(F32)
    return high, middle, rest - middle


def pack_rows(value):
    high, middle, low = split3(jnp.broadcast_to(value, (EXT, BS)))
    row = lax.broadcasted_iota(jnp.int32, (EXT, BS), 0)
    zero = jnp.zeros_like(high)
    rows = jnp.where(row == 0, high, jnp.where(row == 1, middle, jnp.where(row == 2, low, zero)))
    return jnp.concatenate([rows, zero], axis=1).astype(BF16)


def unpack_rows(rows):
    wide = rows.astype(F32)
    return wide[0:1] + (wide[1:2] + wide[2:3])


def project_kernel(place, features, valid, attn, weight_src, weight_tgt, *outs):
    step = pl.program_id(0)
    source = jnp.dot(features[...], weight_src[...], preferred_element_type=F32).astype(BF16)
    target = jnp.dot(features[...], weight_tgt[...], preferred_element_type=F32).astype(BF16)
    linear = jnp.sum(
        source.astype(F32) * attn[pl.ds(step ^ place[0], 1), :], axis=1, keepdims=True
    )
    linear = jnp.broadcast_to(linear, (BS, BS)).T[0:1]
    extra = pack_rows(jnp.where(valid[...] > 0, linear, FLOOR))
    for d, out in enumerate(outs):

        @pl.when(step == d)
        def _():
            out[:BS, :] = source
            out[BS:SRC, :] = extra
            out[SRC:, :] = target


def project(place, features, valid, attn, weight_src, weight_tgt):
    heads = attn.shape[0]
    width = features.shape[1]
    return pl.pallas_call(
        project_kernel,
        grid_spec=pltpu.PrefetchScalarGridSpec(
            num_scalar_prefetch=1,
            grid=(heads,),
            in_specs=[
                pl.BlockSpec((BS, width), lambda d, place: (0, 0)),
                pl.BlockSpec((1, BS), lambda d, place: (0, 0)),
                pl.BlockSpec((heads, HS), lambda d, place: (0, 0)),
                pl.BlockSpec((width, HS), lambda d, place: (0, d ^ place[0])),
                pl.BlockSpec((width, HS), lambda d, place: (0, d ^ place[0])),
            ],
            out_specs=[pl.BlockSpec((ALL, HS), lambda d, place: (0, 0))] * heads,
        ),
        out_shape=[jax.ShapeDtypeStruct((ALL, HS), BF16)] * heads,
        name="project",
    )(place, features, valid, attn, weight_src, weight_tgt)


def gather_kernel(*refs):
    parts, (source, target) = refs[:4], refs[4:]
    for d, part in enumerate(parts):
        source[d] = part[:SRC, :]
        target[d] = part[SRC:, :]


def gather_square(parts):
    return pl.pallas_call(
        gather_kernel,
        out_shape=[
            jax.ShapeDtypeStruct((4, SRC, HS), BF16),
            jax.ShapeDtypeStruct((4, BS, HS), BF16),
        ],
        name="gather_square",
    )(*parts)


def pair_kernel(first, second, out):
    out[:4] = first[...]
    out[4:] = second[...]


def pair(first, second):
    return pl.pallas_call(
        pair_kernel, out_shape=jax.ShapeDtypeStruct((8, *first.shape[1:]), BF16), name="pair"
    )(first, second)


def score_plane(target, minus, wide, halves, scaled, planes):
    lane = lax.broadcasted_iota(jnp.int32, (BS, BS), 1)
    half = BS // 2
    wide[...] = target.astype(F32)
    tiled = wide[...].astype(BF16).reshape(BS // 16, 16, HS)
    weights = halves[...]
    left, right = scaled[:, :BS], scaled[:, BS:]
    waiting = []

    def flush():
        tiles = []
        for u, side in waiting:
            row = minus[u + side * half : u + side * half + 1, :]
            row = jnp.broadcast_to(row, (16, HS)).astype(BF16)
            tiles.append(jnp.maximum(tiled, row[None]).reshape(BS, HS))
        sums = jnp.dot(jnp.concatenate(tiles), weights, preferred_element_type=F32)
        for at, (u, side) in enumerate(waiting):
            pltpu.store(
                planes.at[side], sums[at * BS : (at + 1) * BS], mask=(lane == u) | (lane == u + half)
            )
        waiting.clear()

    for u in range(half):
        for side in range(2):
            if u % 2 == 0:
                waiting.append((u, side))
                if len(waiting) == PER_DOT:
                    flush()
            else:
                s = u + side * half
                row = minus[s : s + 1, :]
                terms = (
                    jnp.maximum(wide[:, :BS], row[:, :BS]) * left
                    + jnp.maximum(wide[:, BS:], row[:, BS:]) * right
                )
                sums = jnp.broadcast_to(jnp.sum(terms, axis=1, keepdims=True), (BS, BS))
                pltpu.store(planes.at[2], sums, mask=lane == s)
    low, high = planes[0], planes[1]
    low = low + pltpu.roll(low, half, 1)
    high = high + pltpu.roll(high, half, 1)
    return jnp.where(lane % 2 == 1, planes[2], jnp.where(lane < half, low, high))


def attend_kernel(kind, split, picked, shift, *refs):
    parts = split[2]
    if kind == "self":
        target_pieces, source_pieces, (masks, halves, scaled, *outs) = refs[:1], refs[1:2], refs[2:]
        outs, (acc, peak, den, minus, wide, planes) = outs[:parts], outs[parts:]
        targets, sources = target_pieces[0], source_pieces[0]
    else:
        count, target_at, source_at, out_at, pick_at, masks, halves, scaled = refs[:8]
        target_pieces, source_pieces = refs[8 : 8 + split[0]], refs[8 + split[0] : 8 + sum(split[:2])]
        rest = refs[8 + sum(split[:2]) :]
        outs, (acc, peak, den, minus, wide, planes, targets, sources, sems) = rest[:parts], rest[parts:]
    blocks = acc.shape[0]
    copies = []
    if kind != "self":
        for pieces, table in ((target_pieces, targets), (source_pieces, sources)):
            at = 0
            for piece in pieces:
                size = piece.shape[0]
                copies.append(
                    pltpu.make_async_copy(piece, table.at[pl.ds(at, size)], sems.at[len(copies)])
                )
                at += size
    for copy in copies:
        copy.start()

    def clear(b, carry):
        acc[b] = jnp.zeros((BS, HS), F32)
        peak[b] = jnp.full((BS, BS), FLOOR, F32)
        den[b] = jnp.zeros((BS, BS), F32)
        return carry

    lax.fori_loop(0, blocks, clear, 0)
    for copy in copies:
        copy.wait()

    def one(cell, slot, a, b, c):
        source = sources[b, :BS, :]
        minus[...] = -source.astype(F32)
        linear = unpack_rows(sources[b, BS:SRC, :BS])
        scores = score_plane(targets[a], minus, wide, halves, scaled[...], planes)
        mask = masks[cell, pl.ds(pl.multiple_of(slot * BS, BS), BS), :].astype(F32)
        if kind == "backward":
            mask = mask.T
        scores = jnp.where(mask > 0, scores + linear, FLOOR)
        before = peak[c]
        top = jnp.maximum(before, jnp.max(scores, axis=1, keepdims=True))
        scale = jnp.exp(before - top)
        weights = jnp.exp(scores - top)
        peak[c] = top
        den[c] = den[c] * scale + jnp.sum(weights, axis=1, keepdims=True)
        acc[c] = acc[c] * jnp.concatenate([scale, scale], axis=1) + jnp.dot(
            weights.astype(BF16), source, preferred_element_type=F32
        )

    if kind == "self":

        def own_step(b, carry):
            one(b, 8, b, b, b)
            return carry

        lax.fori_loop(0, blocks, own_step, 0)
    else:
        ends = [count[0], count[0] + count[1], count[0] + count[1] + count[2]]

        def step(i, carry):
            cell, start = jnp.int32(0), jnp.int32(0)
            for end in ends:
                past = i >= end
                cell = cell + jnp.where(past, 1, 0)
                start = jnp.where(past, end, start)
            slot = i - start
            at = cell * 8 + slot
            pick = pick_at[at]

            @pl.when((pick >= picked[0]) & (pick < picked[1]))
            def _():
                one(cell, slot, target_at[at] - shift, source_at[at], out_at[at] - shift)

            return carry

        lax.fori_loop(0, ends[2] + count[3], step, 0)

    each = blocks // parts
    for part, out in enumerate(outs):

        def finish(at, carry):
            b = part * each + at
            total = jnp.maximum(den[b], 1e-30)
            inverse = 1.0 / total
            out[at, :BS, :] = (acc[b] * jnp.concatenate([inverse, inverse], axis=1)).astype(BF16)
            out[at, BS:, :] = pack_rows((peak[b] + jnp.log(total)).T[0:1])
            return carry

        lax.fori_loop(0, each, finish, 0)


def attend(kind, lists, masks, attn, targets, sources, blocks=4, parts=1, picked=None, shift=0):
    smem = pl.BlockSpec(memory_space=pltpu.SMEM)
    vmem = pl.BlockSpec(memory_space=pltpu.VMEM)
    hbm = pl.BlockSpec(memory_space=pltpu.HBM)
    split = (len(targets), len(sources), parts)
    slots = 4 if kind == "self" else 8
    scratch = [
        pltpu.VMEM((blocks, BS, HS), F32),
        pltpu.VMEM((blocks, BS, BS), F32),
        pltpu.VMEM((blocks, BS, BS), F32),
        pltpu.VMEM((BS, HS), F32),
        pltpu.VMEM((BS, HS), F32),
        pltpu.VMEM((3, BS, BS), F32),
    ]
    if kind == "self":
        operands = (*targets, *sources, masks, *attn)
        specs = [vmem] * 5
    else:
        operands = (*lists, masks, *attn, *targets, *sources)
        specs = [smem] * 5 + [vmem] * 3 + [hbm] * sum(split[:2])
        scratch += [
            pltpu.VMEM((sum(t.shape[0] for t in targets), BS, HS), BF16),
            pltpu.VMEM((sum(t.shape[0] for t in sources), SRC, HS), BF16),
            pltpu.SemaphoreType.DMA((sum(split[:2]),)),
        ]
    return pl.pallas_call(
        functools.partial(attend_kernel, kind, split, picked, shift),
        out_shape=[jax.ShapeDtypeStruct((blocks // parts, SRC, HS), BF16)] * parts,
        in_specs=specs,
        out_specs=[vmem] * parts,
        scratch_shapes=scratch,
        compiler_params=pltpu.CompilerParams(
            vmem_limit_bytes=(16 if kind == "self" else 56) << 20
        ),
        cost_estimate=pl.CostEstimate(
            flops=slots * BS * BS * HS * 512, bytes_accessed=1 << 20, transcendentals=0
        ),
        name="attend_" + kind,
    )(*operands)


def merge_kernel(place, far, *refs):
    *single, bias, out = refs
    parts = [far.at[p, 0] for p in range(8)] + [ref.at[0] for ref in single]
    sums = [unpack_rows(part[BS:SRC, :BS]) for part in parts]
    top = functools.reduce(jnp.maximum, sums)
    shares = [jnp.exp(value - top) for value in sums]
    total = functools.reduce(jnp.add, shares)
    table = jnp.concatenate([share / total for share in shares] + [jnp.zeros((BS - len(parts), BS), F32)])
    table = table.T
    result = jnp.zeros((BS, HS), F32)
    for p, part in enumerate(parts):
        result = result + part[:BS, :].astype(F32) * table[:, p : p + 1]
    out[0] = (result + bias[...]).astype(BF16)


def merge(place, far, single, bias):
    blocks = single[0].shape[0]
    return pl.pallas_call(
        merge_kernel,
        grid_spec=pltpu.PrefetchScalarGridSpec(
            num_scalar_prefetch=1,
            grid=(blocks,),
            in_specs=[pl.BlockSpec((8, 1, SRC, HS), lambda d, place: (0, d, 0, 0))]
            + [pl.BlockSpec((1, SRC, HS), lambda d, place: (d, 0, 0))] * len(single)
            + [pl.BlockSpec((1, HS), lambda d, place: (0, 0))],
            out_specs=pl.BlockSpec((1, BS, HS), lambda d, place: (d ^ place[0], 0, 0)),
        ),
        out_shape=jax.ShapeDtypeStruct((blocks, BS, HS), BF16),
        name="merge",
    )(place, far, *single, bias)


def body(
    features,
    node_valid,
    self_mask,
    pair_blocks,
    pair_count,
    pair_masks,
    weight_src,
    weight_tgt,
    attn,
    bias,
):
    heads = attn.shape[0]
    group = ("rp", "cp")
    row_part, col_part = lax.axis_index("rp"), lax.axis_index("cp")
    head = row_part * 2 + col_part

    place = head.reshape(1)

    def swap(d, value):
        return lax.ppermute(value, group, [(i, i ^ d) for i in range(4)])

    sent = project(place, features, node_valid, attn, weight_src, weight_tgt)
    mine = [sent[0]] + [swap(d, sent[d]) for d in (1, 2, 3)]

    identity = jnp.eye(BS, dtype=bool)
    own_mask = (self_mask[0] > 0) | identity
    first, second = pair_blocks[0, 0, :, 0] % 16, pair_blocks[0, 0, :, 1] // 16
    first_at = (first // 2) * 4 + row_part * 2 + first % 2
    second_at = (second // 2) * 4 + (second % 2) * 2 + col_part
    info = jnp.stack([first_at, second_at, jnp.broadcast_to(pair_count[0, 0], (8,))])
    info = jnp.pad(info, ((0, EXT - 3), (0, BS - 8)))
    cell = jnp.concatenate(
        [
            pair_masks.reshape(8 * BS, BS).astype(BF16),
            own_mask.astype(BF16),
            info.astype(BF16),
        ]
    )
    cells = jnp.stack([cell] + [swap(d, cell) for d in (1, 2, 3)])
    lists = cells[:, 9 * BS : 9 * BS + 3, :8].astype(jnp.int32)
    first_at, second_at = lists[:, 0].reshape(32) ^ head, lists[:, 1].reshape(32) ^ head
    count = lists[:, 2, 0]
    me = lax.axis_index("R")
    from_row = second_at // 4
    y_steps = (me // 2 - from_row // 2) % 4
    x_steps = (me + from_row) % 2
    second_near = ((y_steps + 3) % 4 * 2 + x_steps) * 4 + second_at % 4
    z_steps = (lax.axis_index("C") - first_at // 4) % 8
    first_near = (z_steps + 1) % 8 * 4 + first_at % 4

    source, target = gather_square(mine)

    size = lax.axis_size("R")
    across = [(i, i ^ 1) for i in range(size)]
    around = [[(i, (i + 2 * k) % size) for i in range(size)] for k in (1, 2, 3)]

    def along_z(step, value):
        return lax.ppermute(value, "C", [(i, (i + step) % 8) for i in range(8)])

    row_targets = lax.all_gather(target, "C", axis=0, tiled=True)
    source_beside = lax.ppermute(source, "R", across)
    col_sources = []
    for way in around:
        col_sources += [lax.ppermute(source, "R", way), lax.ppermute(source_beside, "R", way)]
    col_sources += [source, source_beside]
    near_targets = [along_z(7, target), target, along_z(1, target)]
    col_sources, near_targets, later_target = lax.optimization_barrier(
        (col_sources, near_targets, target)
    )
    target_beside = lax.ppermute(later_target, "R", across)

    scaled = 0.8 * lax.dynamic_index_in_dim(attn, head, 0, keepdims=False)
    high = lax.reduce_precision(scaled, 8, 7)
    low = scaled - high
    halves = jnp.concatenate(
        [jnp.broadcast_to(part[:, None], (HS, BS // 2)) for part in (high, low)], axis=1
    ).astype(BF16)
    shared = (halves, scaled[None])

    (own,) = attend("self", (), cells, shared, [target], [source])
    to_near = attend(
        "forward",
        (count, first_near, second_near, first_near, first_near),
        cells,
        shared,
        near_targets,
        col_sources,
        blocks=12,
        parts=3,
        picked=(0, 12),
    )
    both = pair(later_target, target_beside)
    row_targets, both, later_source, own, to_near = lax.optimization_barrier(
        (row_targets, both, source, own, to_near)
    )
    row_sources = lax.all_gather(later_source, "C", axis=0, tiled=True)
    around_targets = [lax.ppermute(both, "R", way) for way in around]
    (to_far,) = attend(
        "forward",
        (count, first_at, second_near, first_at, first_near),
        cells,
        shared,
        [row_targets],
        col_sources,
        blocks=32,
        picked=(12, 32),
    )
    near = [along_z(1, to_near[0]), to_near[1], along_z(7, to_near[2])]
    to_far, around_targets = lax.optimization_barrier((to_far, around_targets))
    far = lax.all_to_all(to_far, "C", 0, 0, tiled=True).reshape(8, 4, SRC, HS)
    cols = []
    for half in range(2):
        to_cols = attend(
            "backward",
            (count, second_near, first_at, second_near, second_near),
            cells,
            shared,
            around_targets[:2] if half == 0 else [around_targets[2], both],
            [row_sources],
            blocks=16,
            parts=4,
            picked=(16 * half, 16 * half + 16),
            shift=16 * half,
        )
        for part, value in enumerate(to_cols):
            y_step, x_step = (1, 2, 3, 0)[half * 2 + part // 2], part % 2
            back = [(i, (i // 2 - y_step) % 4 * 2 + (i % 2 ^ x_step)) for i in range(size)]
            cols.append(value if y_step == x_step == 0 else lax.ppermute(value, "R", back))
    bias_head = lax.dynamic_index_in_dim(bias.reshape(heads, HS), head, 0)
    merged = merge(place, far, [*near, *cols, own], bias_head)
    merged = lax.all_to_all(merged, group, 0, 0, tiled=True)
    result = merged.transpose(1, 0, 2).reshape(BS, heads * HS)
    return jnp.where(node_valid[0][:, None] > 0, result, bias.astype(BF16)[None, :])


def solution(mesh):
    fine = Mesh(mesh.devices.reshape(8, 2, 8, 2), ("R", "rp", "C", "cp"))
    row, col = ("R", "rp"), ("C", "cp")
    both = row + col
    return jax.shard_map(
        body,
        mesh=fine,
        in_specs=(
            P(both, None),
            P(both, None),
            P(both, None, None),
            P(row, col, None, None),
            P(row, col),
            P(row, col, None, None, None),
            P(),
            P(),
            P(),
            P(),
        ),
        out_specs=P(both, None),
        check_vma=False,
    )
```

```python
import functools

import jax
import jax.numpy as jnp
from jax import lax
from jax.experimental import pallas as pl
from jax.experimental.pallas import tpu as pltpu
from jax.sharding import Mesh, PartitionSpec as P

F32 = jnp.float32
BF16 = jnp.bfloat16
FLOOR = -1e30
BS = 128
HS = 256
EXT = 16
SRC = BS + EXT
ALL = SRC + BS
PER_DOT = 4


def split3(value):
    high = value.astype(BF16).astype(F32)
    rest = value - high
    middle = rest.astype(BF16).astype(F32)
    return high, middle, rest - middle


def pack_rows(value):
    high, middle, low = split3(jnp.broadcast_to(value, (EXT, BS)))
    row = lax.broadcasted_iota(jnp.int32, (EXT, BS), 0)
    zero = jnp.zeros_like(high)
    rows = jnp.where(row == 0, high, jnp.where(row == 1, middle, jnp.where(row == 2, low, zero)))
    return jnp.concatenate([rows, zero], axis=1).astype(BF16)


def unpack_rows(rows):
    wide = rows.astype(F32)
    return wide[0:1] + (wide[1:2] + wide[2:3])


def project_kernel(place, features, valid, attn, weight_src, weight_tgt, *outs):
    step = pl.program_id(0)
    source = jnp.dot(features[...], weight_src[...], preferred_element_type=F32).astype(BF16)
    target = jnp.dot(features[...], weight_tgt[...], preferred_element_type=F32).astype(BF16)
    linear = jnp.sum(
        source.astype(F32) * attn[pl.ds(step ^ place[0], 1), :], axis=1, keepdims=True
    )
    linear = jnp.broadcast_to(linear, (BS, BS)).T[0:1]
    extra = pack_rows(jnp.where(valid[...] > 0, linear, FLOOR))
    for d, out in enumerate(outs):

        @pl.when(step == d)
        def _():
            out[:BS, :] = source
            out[BS:SRC, :] = extra
            out[SRC:, :] = target


def project(place, features, valid, attn, weight_src, weight_tgt):
    heads = attn.shape[0]
    width = features.shape[1]
    return pl.pallas_call(
        project_kernel,
        grid_spec=pltpu.PrefetchScalarGridSpec(
            num_scalar_prefetch=1,
            grid=(heads,),
            in_specs=[
                pl.BlockSpec((BS, width), lambda d, place: (0, 0)),
                pl.BlockSpec((1, BS), lambda d, place: (0, 0)),
                pl.BlockSpec((heads, HS), lambda d, place: (0, 0)),
                pl.BlockSpec((width, HS), lambda d, place: (0, d ^ place[0])),
                pl.BlockSpec((width, HS), lambda d, place: (0, d ^ place[0])),
            ],
            out_specs=[pl.BlockSpec((ALL, HS), lambda d, place: (0, 0))] * heads,
        ),
        out_shape=[jax.ShapeDtypeStruct((ALL, HS), BF16)] * heads,
        name="project",
    )(place, features, valid, attn, weight_src, weight_tgt)


def gather_kernel(*refs):
    parts, (source, target) = refs[:4], refs[4:]
    for d, part in enumerate(parts):
        source[d] = part[:SRC, :]
        target[d] = part[SRC:, :]


def gather_square(parts):
    return pl.pallas_call(
        gather_kernel,
        out_shape=[
            jax.ShapeDtypeStruct((4, SRC, HS), BF16),
            jax.ShapeDtypeStruct((4, BS, HS), BF16),
        ],
        name="gather_square",
    )(*parts)


def pair_kernel(first, second, out):
    out[:4] = first[...]
    out[4:] = second[...]


def pair(first, second):
    return pl.pallas_call(
        pair_kernel, out_shape=jax.ShapeDtypeStruct((8, *first.shape[1:]), BF16), name="pair"
    )(first, second)


def score_plane(target, minus, wide, halves, scaled, planes):
    lane = lax.broadcasted_iota(jnp.int32, (BS, BS), 1)
    half = BS // 2
    wide[...] = target.astype(F32)
    tiled = wide[...].astype(BF16).reshape(BS // 16, 16, HS)
    weights = halves[...]
    left, right = scaled[:, :BS], scaled[:, BS:]
    waiting = []

    def flush():
        tiles = []
        for u, side in waiting:
            row = minus[u + side * half : u + side * half + 1, :]
            row = jnp.broadcast_to(row, (16, HS)).astype(BF16)
            tiles.append(jnp.maximum(tiled, row[None]).reshape(BS, HS))
        sums = jnp.dot(jnp.concatenate(tiles), weights, preferred_element_type=F32)
        for at, (u, side) in enumerate(waiting):
            pltpu.store(
                planes.at[side], sums[at * BS : (at + 1) * BS], mask=(lane == u) | (lane == u + half)
            )
        waiting.clear()

    for u in range(half):
        for side in range(2):
            if u % 2 == 0:
                waiting.append((u, side))
                if len(waiting) == PER_DOT:
                    flush()
            else:
                s = u + side * half
                row = minus[s : s + 1, :]
                terms = (
                    jnp.maximum(wide[:, :BS], row[:, :BS]) * left
                    + jnp.maximum(wide[:, BS:], row[:, BS:]) * right
                )
                sums = jnp.broadcast_to(jnp.sum(terms, axis=1, keepdims=True), (BS, BS))
                pltpu.store(planes.at[2], sums, mask=lane == s)
    low, high = planes[0], planes[1]
    low = low + pltpu.roll(low, half, 1)
    high = high + pltpu.roll(high, half, 1)
    return jnp.where(lane % 2 == 1, planes[2], jnp.where(lane < half, low, high))


def attend_kernel(kind, split, picked, shift, *refs):
    parts = split[2]
    if kind == "self":
        target_pieces, source_pieces, (masks, halves, scaled, *outs) = refs[:1], refs[1:2], refs[2:]
        outs, (acc, peak, den, minus, wide, planes) = outs[:parts], outs[parts:]
        targets, sources = target_pieces[0], source_pieces[0]
    else:
        count, target_at, source_at, out_at, pick_at, masks, halves, scaled = refs[:8]
        target_pieces, source_pieces = refs[8 : 8 + split[0]], refs[8 + split[0] : 8 + sum(split[:2])]
        rest = refs[8 + sum(split[:2]) :]
        outs, (acc, peak, den, minus, wide, planes, targets, sources, sems) = rest[:parts], rest[parts:]
    blocks = acc.shape[0]
    copies = []
    if kind != "self":
        for pieces, table in ((target_pieces, targets), (source_pieces, sources)):
            at = 0
            for piece in pieces:
                size = piece.shape[0]
                copies.append(
                    pltpu.make_async_copy(piece, table.at[pl.ds(at, size)], sems.at[len(copies)])
                )
                at += size
    for copy in copies:
        copy.start()

    def clear(b, carry):
        acc[b] = jnp.zeros((BS, HS), F32)
        peak[b] = jnp.full((BS, BS), FLOOR, F32)
        den[b] = jnp.zeros((BS, BS), F32)
        return carry

    lax.fori_loop(0, blocks, clear, 0, unroll=4)
    for copy in copies:
        copy.wait()

    def one(cell, slot, a, b, c):
        source = sources[b, :BS, :]
        minus[...] = -source.astype(F32)
        linear = unpack_rows(sources[b, BS:SRC, :BS])
        scores = score_plane(targets[a], minus, wide, halves, scaled[...], planes)
        mask = masks[cell, pl.ds(pl.multiple_of(slot * BS, BS), BS), :].astype(F32)
        if kind == "backward":
            mask = mask.T
        scores = jnp.where(mask > 0, scores + linear, FLOOR)
        before = peak[c]
        top = jnp.maximum(before, jnp.max(scores, axis=1, keepdims=True))
        scale = jnp.exp(before - top)
        weights = jnp.exp(scores - top)
        peak[c] = top
        den[c] = den[c] * scale + jnp.sum(weights, axis=1, keepdims=True)
        acc[c] = acc[c] * jnp.concatenate([scale, scale], axis=1) + jnp.dot(
            weights.astype(BF16), source, preferred_element_type=F32
        )

    if kind == "self":

        def own_step(b, carry):
            one(b, 8, b, b, b)
            return carry

        lax.fori_loop(0, blocks, own_step, 0)
    else:
        ends = [count[0], count[0] + count[1], count[0] + count[1] + count[2]]

        def step(i, carry):
            cell, start = jnp.int32(0), jnp.int32(0)
            for end in ends:
                past = i >= end
                cell = cell + jnp.where(past, 1, 0)
                start = jnp.where(past, end, start)
            slot = i - start
            at = cell * 8 + slot
            pick = pick_at[at]

            @pl.when((pick >= picked[0]) & (pick < picked[1]))
            def _():
                one(cell, slot, target_at[at] - shift, source_at[at], out_at[at] - shift)

            return carry

        lax.fori_loop(0, ends[2] + count[3], step, 0)

    each = blocks // parts
    for part, out in enumerate(outs):

        def finish(at, carry):
            b = part * each + at
            total = jnp.maximum(den[b], 1e-30)
            inverse = 1.0 / total
            out[at, :BS, :] = (acc[b] * jnp.concatenate([inverse, inverse], axis=1)).astype(BF16)
            out[at, BS:, :] = pack_rows((peak[b] + jnp.log(total)).T[0:1])
            return carry

        lax.fori_loop(0, each, finish, 0, unroll=4)


def attend(kind, lists, masks, attn, targets, sources, blocks=4, parts=1, picked=None, shift=0):
    smem = pl.BlockSpec(memory_space=pltpu.SMEM)
    vmem = pl.BlockSpec(memory_space=pltpu.VMEM)
    hbm = pl.BlockSpec(memory_space=pltpu.HBM)
    split = (len(targets), len(sources), parts)
    slots = 4 if kind == "self" else 8
    scratch = [
        pltpu.VMEM((blocks, BS, HS), F32),
        pltpu.VMEM((blocks, BS, BS), F32),
        pltpu.VMEM((blocks, BS, BS), F32),
        pltpu.VMEM((BS, HS), F32),
        pltpu.VMEM((BS, HS), F32),
        pltpu.VMEM((3, BS, BS), F32),
    ]
    if kind == "self":
        operands = (*targets, *sources, masks, *attn)
        specs = [vmem] * 5
    else:
        operands = (*lists, masks, *attn, *targets, *sources)
        specs = [smem] * 5 + [vmem] * 3 + [hbm] * sum(split[:2])
        scratch += [
            pltpu.VMEM((sum(t.shape[0] for t in targets), BS, HS), BF16),
            pltpu.VMEM((sum(t.shape[0] for t in sources), SRC, HS), BF16),
            pltpu.SemaphoreType.DMA((sum(split[:2]),)),
        ]
    return pl.pallas_call(
        functools.partial(attend_kernel, kind, split, picked, shift),
        out_shape=[jax.ShapeDtypeStruct((blocks // parts, SRC, HS), BF16)] * parts,
        in_specs=specs,
        out_specs=[vmem] * parts,
        scratch_shapes=scratch,
        compiler_params=pltpu.CompilerParams(
            vmem_limit_bytes=(16 if kind == "self" else 56) << 20
        ),
        cost_estimate=pl.CostEstimate(
            flops=slots * BS * BS * HS * 512, bytes_accessed=1 << 20, transcendentals=0
        ),
        name="attend_" + kind,
    )(*operands)


def merge_kernel(place, far, *refs):
    *single, bias, out = refs
    parts = [far.at[p, 0] for p in range(8)] + [ref.at[0] for ref in single]
    sums = [unpack_rows(part[BS:SRC, :BS]) for part in parts]
    top = functools.reduce(jnp.maximum, sums)
    shares = [jnp.exp(value - top) for value in sums]
    total = functools.reduce(jnp.add, shares)
    table = jnp.concatenate([share / total for share in shares] + [jnp.zeros((BS - len(parts), BS), F32)])
    table = table.T
    result = jnp.zeros((BS, HS), F32)
    for p, part in enumerate(parts):
        result = result + part[:BS, :].astype(F32) * table[:, p : p + 1]
    out[0] = (result + bias[...]).astype(BF16)


def merge(place, far, single, bias):
    blocks = single[0].shape[0]
    return pl.pallas_call(
        merge_kernel,
        grid_spec=pltpu.PrefetchScalarGridSpec(
            num_scalar_prefetch=1,
            grid=(blocks,),
            in_specs=[pl.BlockSpec((8, 1, SRC, HS), lambda d, place: (0, d, 0, 0))]
            + [pl.BlockSpec((1, SRC, HS), lambda d, place: (d, 0, 0))] * len(single)
            + [pl.BlockSpec((1, HS), lambda d, place: (0, 0))],
            out_specs=pl.BlockSpec((1, BS, HS), lambda d, place: (d ^ place[0], 0, 0)),
        ),
        out_shape=jax.ShapeDtypeStruct((blocks, BS, HS), BF16),
        name="merge",
    )(place, far, *single, bias)


def body(
    features,
    node_valid,
    self_mask,
    pair_blocks,
    pair_count,
    pair_masks,
    weight_src,
    weight_tgt,
    attn,
    bias,
):
    heads = attn.shape[0]
    group = ("rp", "cp")
    row_part, col_part = lax.axis_index("rp"), lax.axis_index("cp")
    head = row_part * 2 + col_part

    place = head.reshape(1)

    def swap(d, value):
        return lax.ppermute(value, group, [(i, i ^ d) for i in range(4)])

    sent = project(place, features, node_valid, attn, weight_src, weight_tgt)
    mine = [sent[0]] + [swap(d, sent[d]) for d in (1, 2, 3)]

    identity = jnp.eye(BS, dtype=bool)
    own_mask = (self_mask[0] > 0) | identity
    first, second = pair_blocks[0, 0, :, 0] % 16, pair_blocks[0, 0, :, 1] // 16
    first_at = (first // 2) * 4 + row_part * 2 + first % 2
    second_at = (second // 2) * 4 + (second % 2) * 2 + col_part
    info = jnp.stack([first_at, second_at, jnp.broadcast_to(pair_count[0, 0], (8,))])
    info = jnp.pad(info, ((0, EXT - 3), (0, BS - 8)))
    cell = jnp.concatenate(
        [
            pair_masks.reshape(8 * BS, BS).astype(BF16),
            own_mask.astype(BF16),
            info.astype(BF16),
        ]
    )
    cells = jnp.stack([cell] + [swap(d, cell) for d in (1, 2, 3)])
    lists = cells[:, 9 * BS : 9 * BS + 3, :8].astype(jnp.int32)
    first_at, second_at = lists[:, 0].reshape(32) ^ head, lists[:, 1].reshape(32) ^ head
    count = lists[:, 2, 0]
    me = lax.axis_index("R")
    from_row = second_at // 4
    y_steps = (me // 2 - from_row // 2) % 4
    x_steps = (me + from_row) % 2
    second_near = ((y_steps + 3) % 4 * 2 + x_steps) * 4 + second_at % 4
    z_steps = (lax.axis_index("C") - first_at // 4) % 8
    first_near = (z_steps + 1) % 8 * 4 + first_at % 4

    source, target = gather_square(mine)

    size = lax.axis_size("R")
    across = [(i, i ^ 1) for i in range(size)]
    around = [[(i, (i + 2 * k) % size) for i in range(size)] for k in (1, 2, 3)]

    def along_z(step, value):
        return lax.ppermute(value, "C", [(i, (i + step) % 8) for i in range(8)])

    row_targets = lax.all_gather(target, "C", axis=0, tiled=True)
    source_beside = lax.ppermute(source, "R", across)
    col_sources = []
    for way in around:
        col_sources += [lax.ppermute(source, "R", way), lax.ppermute(source_beside, "R", way)]
    col_sources += [source, source_beside]
    near_targets = [along_z(7, target), target, along_z(1, target)]
    col_sources, near_targets, later_target = lax.optimization_barrier(
        (col_sources, near_targets, target)
    )
    target_beside = lax.ppermute(later_target, "R", across)

    scaled = 0.8 * lax.dynamic_index_in_dim(attn, head, 0, keepdims=False)
    high = lax.reduce_precision(scaled, 8, 7)
    low = scaled - high
    halves = jnp.concatenate(
        [jnp.broadcast_to(part[:, None], (HS, BS // 2)) for part in (high, low)], axis=1
    ).astype(BF16)
    shared = (halves, scaled[None])

    to_near = attend(
        "forward",
        (count, first_near, second_near, first_near, first_near),
        cells,
        shared,
        near_targets,
        col_sources,
        blocks=12,
        parts=3,
        picked=(0, 12),
    )
    both = pair(later_target, target_beside)
    row_targets, both, later_source, to_near = lax.optimization_barrier(
        (row_targets, both, source, to_near)
    )
    row_sources = lax.all_gather(later_source, "C", axis=0, tiled=True)
    around_targets = [lax.ppermute(both, "R", way) for way in around]
    (to_far,) = attend(
        "forward",
        (count, first_at, second_near, first_at, first_near),
        cells,
        shared,
        [row_targets],
        col_sources,
        blocks=32,
        picked=(12, 32),
    )
    near = [along_z(1, to_near[0]), to_near[1], along_z(7, to_near[2])]
    to_far, around_targets = lax.optimization_barrier((to_far, around_targets))
    far = lax.all_to_all(to_far, "C", 0, 0, tiled=True).reshape(8, 4, SRC, HS)
    cols, column_targets = [], [around_targets[:2], [around_targets[2], both]]
    for half in range(2):
        to_cols = attend(
            "backward",
            (count, second_near, first_at, second_near, second_near),
            cells,
            shared,
            column_targets[half],
            [row_sources],
            blocks=16,
            parts=4,
            picked=(16 * half, 16 * half + 16),
            shift=16 * half,
        )
        to_cols, near, cols, column_targets[1] = lax.optimization_barrier(
            (to_cols, near, cols, column_targets[1])
        )
        for part, value in enumerate(to_cols):
            y_step, x_step = (1, 2, 3, 0)[half * 2 + part // 2], part % 2
            back = [(i, (i // 2 - y_step) % 4 * 2 + (i % 2 ^ x_step)) for i in range(size)]
            cols.append(value if y_step == x_step == 0 else lax.ppermute(value, "R", back))
    target, to_cols = lax.optimization_barrier((target, to_cols))
    (own,) = attend("self", (), cells, shared, [target], [source])
    bias_head = lax.dynamic_index_in_dim(bias.reshape(heads, HS), head, 0)
    merged = merge(place, far, [*near, *cols, own], bias_head)
    merged = lax.all_to_all(merged, group, 0, 0, tiled=True)
    result = merged.transpose(1, 0, 2).reshape(BS, heads * HS)
    return jnp.where(node_valid[0][:, None] > 0, result, bias.astype(BF16)[None, :])


def solution(mesh):
    fine = Mesh(mesh.devices.reshape(8, 2, 8, 2), ("R", "rp", "C", "cp"))
    row, col = ("R", "rp"), ("C", "cp")
    both = row + col
    return jax.shard_map(
        body,
        mesh=fine,
        in_specs=(
            P(both, None),
            P(both, None),
            P(both, None, None),
            P(row, col, None, None),
            P(row, col),
            P(row, col, None, None, None),
            P(),
            P(),
            P(),
            P(),
        ),
        out_specs=P(both, None),
        check_vma=False,
    )
```

```python
import functools

import jax
import jax.numpy as jnp
from jax import lax
from jax.experimental import pallas as pl
from jax.experimental.pallas import tpu as pltpu
from jax.sharding import Mesh, PartitionSpec as P

F32 = jnp.float32
BF16 = jnp.bfloat16
FLOOR = -1e30
BS = 128
HS = 256
EXT = 16
SRC = BS + EXT
ALL = SRC + BS
PER_DOT = 4


def split3(value):
    high = value.astype(BF16).astype(F32)
    rest = value - high
    middle = rest.astype(BF16).astype(F32)
    return high, middle, rest - middle


def pack_rows(value):
    high, middle, low = split3(jnp.broadcast_to(value, (EXT, BS)))
    row = lax.broadcasted_iota(jnp.int32, (EXT, BS), 0)
    zero = jnp.zeros_like(high)
    rows = jnp.where(row == 0, high, jnp.where(row == 1, middle, jnp.where(row == 2, low, zero)))
    return jnp.concatenate([rows, zero], axis=1).astype(BF16)


def unpack_rows(rows):
    wide = rows.astype(F32)
    return wide[0:1] + (wide[1:2] + wide[2:3])


def project_kernel(place, features, valid, attn, weight_src, weight_tgt, *outs):
    step = pl.program_id(0)
    source = jnp.dot(features[...], weight_src[...], preferred_element_type=F32).astype(BF16)
    target = jnp.dot(features[...], weight_tgt[...], preferred_element_type=F32).astype(BF16)
    linear = jnp.sum(
        source.astype(F32) * attn[pl.ds(step ^ place[0], 1), :], axis=1, keepdims=True
    )
    linear = jnp.broadcast_to(linear, (BS, BS)).T[0:1]
    extra = pack_rows(jnp.where(valid[...] > 0, linear, FLOOR))
    for d, out in enumerate(outs):

        @pl.when(step == d)
        def _():
            out[:BS, :] = source
            out[BS:SRC, :] = extra
            out[SRC:, :] = target


def project(place, features, valid, attn, weight_src, weight_tgt):
    heads = attn.shape[0]
    width = features.shape[1]
    return pl.pallas_call(
        project_kernel,
        grid_spec=pltpu.PrefetchScalarGridSpec(
            num_scalar_prefetch=1,
            grid=(heads,),
            in_specs=[
                pl.BlockSpec((BS, width), lambda d, place: (0, 0)),
                pl.BlockSpec((1, BS), lambda d, place: (0, 0)),
                pl.BlockSpec((heads, HS), lambda d, place: (0, 0)),
                pl.BlockSpec((width, HS), lambda d, place: (0, d ^ place[0])),
                pl.BlockSpec((width, HS), lambda d, place: (0, d ^ place[0])),
            ],
            out_specs=[pl.BlockSpec((ALL, HS), lambda d, place: (0, 0))] * heads,
        ),
        out_shape=[jax.ShapeDtypeStruct((ALL, HS), BF16)] * heads,
        name="project",
    )(place, features, valid, attn, weight_src, weight_tgt)


def gather_kernel(*refs):
    parts, (source, target) = refs[:4], refs[4:]
    for d, part in enumerate(parts):
        source[d] = part[:SRC, :]
        target[d] = part[SRC:, :]


def gather_square(parts):
    return pl.pallas_call(
        gather_kernel,
        out_shape=[
            jax.ShapeDtypeStruct((4, SRC, HS), BF16),
            jax.ShapeDtypeStruct((4, BS, HS), BF16),
        ],
        name="gather_square",
    )(*parts)


def pair_kernel(first, second, out):
    out[:4] = first[...]
    out[4:] = second[...]


def pair(first, second):
    return pl.pallas_call(
        pair_kernel, out_shape=jax.ShapeDtypeStruct((8, *first.shape[1:]), BF16), name="pair"
    )(first, second)


def score_plane(target, minus, wide, halves, scaled, planes):
    lane = lax.broadcasted_iota(jnp.int32, (BS, BS), 1)
    half = BS // 2
    wide[...] = target.astype(F32)
    tiled = wide[...].astype(BF16).reshape(BS // 16, 16, HS)
    weights = halves[...]
    left, right = scaled[:, :BS], scaled[:, BS:]
    waiting = []

    def flush():
        tiles = []
        for u, side in waiting:
            row = minus[u + side * half : u + side * half + 1, :]
            row = jnp.broadcast_to(row, (16, HS)).astype(BF16)
            tiles.append(jnp.maximum(tiled, row[None]).reshape(BS, HS))
        sums = jnp.dot(jnp.concatenate(tiles), weights, preferred_element_type=F32)
        for at, (u, side) in enumerate(waiting):
            pltpu.store(
                planes.at[side], sums[at * BS : (at + 1) * BS], mask=(lane == u) | (lane == u + half)
            )
        waiting.clear()

    for u in range(half):
        for side in range(2):
            if u % 2 == 0:
                waiting.append((u, side))
                if len(waiting) == PER_DOT:
                    flush()
            else:
                s = u + side * half
                row = minus[s : s + 1, :]
                terms = (
                    jnp.maximum(wide[:, :BS], row[:, :BS]) * left
                    + jnp.maximum(wide[:, BS:], row[:, BS:]) * right
                )
                sums = jnp.broadcast_to(jnp.sum(terms, axis=1, keepdims=True), (BS, BS))
                pltpu.store(planes.at[2], sums, mask=lane == s)
    low, high = planes[0], planes[1]
    low = low + pltpu.roll(low, half, 1)
    high = high + pltpu.roll(high, half, 1)
    return jnp.where(lane % 2 == 1, planes[2], jnp.where(lane < half, low, high))


def attend_kernel(kind, split, picked, shift, *refs):
    parts = split[2]
    if kind == "self":
        target_pieces, source_pieces, (masks, halves, scaled, *outs) = refs[:1], refs[1:2], refs[2:]
        outs, (acc, peak, den, minus, wide, planes) = outs[:parts], outs[parts:]
        targets, sources = target_pieces[0], source_pieces[0]
    else:
        count, target_at, source_at, out_at, pick_at, masks, halves, scaled = refs[:8]
        target_pieces, source_pieces = refs[8 : 8 + split[0]], refs[8 + split[0] : 8 + sum(split[:2])]
        rest = refs[8 + sum(split[:2]) :]
        outs, (acc, peak, den, minus, wide, planes, targets, sources, sems) = rest[:parts], rest[parts:]
    blocks = acc.shape[0]
    copies = []
    if kind != "self":
        for pieces, table in ((target_pieces, targets), (source_pieces, sources)):
            at = 0
            for piece in pieces:
                size = piece.shape[0]
                copies.append(
                    pltpu.make_async_copy(piece, table.at[pl.ds(at, size)], sems.at[len(copies)])
                )
                at += size
    for copy in copies:
        copy.start()

    def clear(b, carry):
        acc[b] = jnp.zeros((BS, HS), F32)
        peak[b] = jnp.full((BS, BS), FLOOR, F32)
        den[b] = jnp.zeros((BS, BS), F32)
        return carry

    lax.fori_loop(0, blocks, clear, 0, unroll=4)
    for copy in copies:
        copy.wait()

    def one(cell, slot, a, b, c):
        source = sources[b, :BS, :]
        minus[...] = -source.astype(F32)
        linear = unpack_rows(sources[b, BS:SRC, :BS])
        scores = score_plane(targets[a], minus, wide, halves, scaled[...], planes)
        mask = masks[cell, pl.ds(pl.multiple_of(slot * BS, BS), BS), :].astype(F32)
        if kind == "backward":
            mask = mask.T
        scores = jnp.where(mask > 0, scores + linear, FLOOR)
        before = peak[c]
        top = jnp.maximum(before, jnp.max(scores, axis=1, keepdims=True))
        scale = jnp.exp(before - top)
        weights = jnp.exp(scores - top)
        peak[c] = top
        den[c] = den[c] * scale + jnp.sum(weights, axis=1, keepdims=True)
        acc[c] = acc[c] * jnp.concatenate([scale, scale], axis=1) + jnp.dot(
            weights.astype(BF16), source, preferred_element_type=F32
        )

    if kind == "self":

        def own_step(b, carry):
            one(b, 8, b, b, b)
            return carry

        lax.fori_loop(0, blocks, own_step, 0)
    else:
        ends = [count[0], count[0] + count[1], count[0] + count[1] + count[2]]

        def step(i, carry):
            cell, start = jnp.int32(0), jnp.int32(0)
            for end in ends:
                past = i >= end
                cell = cell + jnp.where(past, 1, 0)
                start = jnp.where(past, end, start)
            slot = i - start
            at = cell * 8 + slot
            pick = pick_at[at]

            @pl.when((pick >= picked[0]) & (pick < picked[1]))
            def _():
                one(cell, slot, target_at[at] - shift, source_at[at], out_at[at] - shift)

            return carry

        lax.fori_loop(0, ends[2] + count[3], step, 0)

    each = blocks // parts
    for part, out in enumerate(outs):

        def finish(at, carry):
            b = part * each + at
            total = jnp.maximum(den[b], 1e-30)
            inverse = 1.0 / total
            out[at, :BS, :] = (acc[b] * jnp.concatenate([inverse, inverse], axis=1)).astype(BF16)
            out[at, BS:, :] = pack_rows((peak[b] + jnp.log(total)).T[0:1])
            return carry

        lax.fori_loop(0, each, finish, 0, unroll=4)


def attend(kind, lists, masks, attn, targets, sources, blocks=4, parts=1, picked=None, shift=0):
    smem = pl.BlockSpec(memory_space=pltpu.SMEM)
    vmem = pl.BlockSpec(memory_space=pltpu.VMEM)
    hbm = pl.BlockSpec(memory_space=pltpu.HBM)
    split = (len(targets), len(sources), parts)
    slots = 4 if kind == "self" else 8
    scratch = [
        pltpu.VMEM((blocks, BS, HS), F32),
        pltpu.VMEM((blocks, BS, BS), F32),
        pltpu.VMEM((blocks, BS, BS), F32),
        pltpu.VMEM((BS, HS), F32),
        pltpu.VMEM((BS, HS), F32),
        pltpu.VMEM((3, BS, BS), F32),
    ]
    if kind == "self":
        operands = (*targets, *sources, masks, *attn)
        specs = [vmem] * 5
    else:
        operands = (*lists, masks, *attn, *targets, *sources)
        specs = [smem] * 5 + [vmem] * 3 + [hbm] * sum(split[:2])
        scratch += [
            pltpu.VMEM((sum(t.shape[0] for t in targets), BS, HS), BF16),
            pltpu.VMEM((sum(t.shape[0] for t in sources), SRC, HS), BF16),
            pltpu.SemaphoreType.DMA((sum(split[:2]),)),
        ]
    return pl.pallas_call(
        functools.partial(attend_kernel, kind, split, picked, shift),
        out_shape=[jax.ShapeDtypeStruct((blocks // parts, SRC, HS), BF16)] * parts,
        in_specs=specs,
        out_specs=[vmem] * parts,
        scratch_shapes=scratch,
        compiler_params=pltpu.CompilerParams(
            vmem_limit_bytes=(16 if kind == "self" else 56) << 20
        ),
        cost_estimate=pl.CostEstimate(
            flops=slots * BS * BS * HS * 512, bytes_accessed=1 << 20, transcendentals=0
        ),
        name="attend_" + kind,
    )(*operands)


def merge_kernel(place, far, *refs):
    *single, bias, out = refs
    parts = [far.at[p, 0] for p in range(8)] + [ref.at[0] for ref in single]
    sums = [unpack_rows(part[BS:SRC, :BS]) for part in parts]
    top = functools.reduce(jnp.maximum, sums)
    shares = [jnp.exp(value - top) for value in sums]
    total = functools.reduce(jnp.add, shares)
    table = jnp.concatenate([share / total for share in shares] + [jnp.zeros((BS - len(parts), BS), F32)])
    table = table.T
    result = jnp.zeros((BS, HS), F32)
    for p, part in enumerate(parts):
        result = result + part[:BS, :].astype(F32) * table[:, p : p + 1]
    out[0] = (result + bias[...]).astype(BF16)


def merge(place, far, single, bias):
    blocks = single[0].shape[0]
    return pl.pallas_call(
        merge_kernel,
        grid_spec=pltpu.PrefetchScalarGridSpec(
            num_scalar_prefetch=1,
            grid=(blocks,),
            in_specs=[pl.BlockSpec((8, 1, SRC, HS), lambda d, place: (0, d, 0, 0))]
            + [pl.BlockSpec((1, SRC, HS), lambda d, place: (d, 0, 0))] * len(single)
            + [pl.BlockSpec((1, HS), lambda d, place: (0, 0))],
            out_specs=pl.BlockSpec((1, BS, HS), lambda d, place: (d ^ place[0], 0, 0)),
        ),
        out_shape=jax.ShapeDtypeStruct((blocks, BS, HS), BF16),
        name="merge",
    )(place, far, *single, bias)


def body(
    features,
    node_valid,
    self_mask,
    pair_blocks,
    pair_count,
    pair_masks,
    weight_src,
    weight_tgt,
    attn,
    bias,
):
    heads = attn.shape[0]
    group = ("rp", "cp")
    row_part, col_part = lax.axis_index("rp"), lax.axis_index("cp")
    head = row_part * 2 + col_part

    place = head.reshape(1)

    def swap(d, value):
        return lax.ppermute(value, group, [(i, i ^ d) for i in range(4)])

    sent = project(place, features, node_valid, attn, weight_src, weight_tgt)
    mine = [sent[0]] + [swap(d, sent[d]) for d in (1, 2, 3)]

    identity = jnp.eye(BS, dtype=bool)
    own_mask = (self_mask[0] > 0) | identity
    first, second = pair_blocks[0, 0, :, 0] % 16, pair_blocks[0, 0, :, 1] // 16
    first_at = (first // 2) * 4 + row_part * 2 + first % 2
    second_at = (second // 2) * 4 + (second % 2) * 2 + col_part
    info = jnp.stack([first_at, second_at, jnp.broadcast_to(pair_count[0, 0], (8,))])
    info = jnp.pad(info, ((0, EXT - 3), (0, BS - 8)))
    cell = jnp.concatenate(
        [
            pair_masks.reshape(8 * BS, BS).astype(BF16),
            own_mask.astype(BF16),
            info.astype(BF16),
        ]
    )
    cells = jnp.stack([cell] + [swap(d, cell) for d in (1, 2, 3)])
    lists = cells[:, 9 * BS : 9 * BS + 3, :8].astype(jnp.int32)
    first_at, second_at = lists[:, 0].reshape(32) ^ head, lists[:, 1].reshape(32) ^ head
    count = lists[:, 2, 0]
    me = lax.axis_index("R")
    from_row = second_at // 4
    y_steps = (me // 2 - from_row // 2) % 4
    x_steps = (me + from_row) % 2
    second_near = ((y_steps + 3) % 4 * 2 + x_steps) * 4 + second_at % 4

    source, target = gather_square(mine)

    size = lax.axis_size("R")
    across = [(i, i ^ 1) for i in range(size)]
    around = [[(i, (i + 2 * k) % size) for i in range(size)] for k in (1, 2, 3)]

    row_targets = lax.all_gather(target, "C", axis=0, tiled=True)
    source_beside = lax.ppermute(source, "R", across)
    source_beside, later_target = lax.optimization_barrier((source_beside, target))
    col_sources = []
    for way in around:
        col_sources += [lax.ppermute(source, "R", way), lax.ppermute(source_beside, "R", way)]
    col_sources += [source, source_beside]
    target_beside = lax.ppermute(later_target, "R", across)

    scaled = 0.8 * lax.dynamic_index_in_dim(attn, head, 0, keepdims=False)
    high = lax.reduce_precision(scaled, 8, 7)
    low = scaled - high
    halves = jnp.concatenate(
        [jnp.broadcast_to(part[:, None], (HS, BS // 2)) for part in (high, low)], axis=1
    ).astype(BF16)
    shared = (halves, scaled[None])

    both = pair(later_target, target_beside)
    lists = (count, first_at, second_near, second_at)
    row_targets, both, later_source, col_sources, cells, shared, lists = lax.optimization_barrier(
        (row_targets, both, source, col_sources, cells, shared, lists)
    )
    count, first_at, second_near, second_at = lists
    row_sources = lax.all_gather(later_source, "C", axis=0, tiled=True)
    around_targets = [lax.ppermute(both, "R", way) for way in around]
    (to_far,) = attend(
        "forward",
        (count, first_at, second_near, first_at, first_at),
        cells,
        shared,
        [row_targets],
        col_sources,
        blocks=32,
        picked=(0, 32),
    )
    to_far, around_targets = lax.optimization_barrier((to_far, around_targets))
    far = lax.all_to_all(to_far, "C", 0, 0, tiled=True).reshape(8, 4, SRC, HS)
    cols, column_targets = [], [around_targets[:2], [around_targets[2], both]]
    for half in range(2):
        to_cols = attend(
            "backward",
            (count, second_near, first_at, second_near, second_near),
            cells,
            shared,
            column_targets[half],
            [row_sources],
            blocks=16,
            parts=4,
            picked=(16 * half, 16 * half + 16),
            shift=16 * half,
        )
        to_cols, cols, column_targets[1] = lax.optimization_barrier(
            (to_cols, cols, column_targets[1])
        )
        for part, value in enumerate(to_cols):
            y_step, x_step = (1, 2, 3, 0)[half * 2 + part // 2], part % 2
            back = [(i, (i // 2 - y_step) % 4 * 2 + (i % 2 ^ x_step)) for i in range(size)]
            cols.append(value if y_step == x_step == 0 else lax.ppermute(value, "R", back))
    target, to_cols = lax.optimization_barrier((target, to_cols))
    (own,) = attend("self", (), cells, shared, [target], [source])
    bias_head = lax.dynamic_index_in_dim(bias.reshape(heads, HS), head, 0)
    merged = merge(place, far, [*cols, own], bias_head)
    merged = lax.all_to_all(merged, group, 0, 0, tiled=True)
    result = merged.transpose(1, 0, 2).reshape(BS, heads * HS)
    return jnp.where(node_valid[0][:, None] > 0, result, bias.astype(BF16)[None, :])


def solution(mesh):
    fine = Mesh(mesh.devices.reshape(8, 2, 8, 2), ("R", "rp", "C", "cp"))
    row, col = ("R", "rp"), ("C", "cp")
    both = row + col
    return jax.shard_map(
        body,
        mesh=fine,
        in_specs=(
            P(both, None),
            P(both, None),
            P(both, None, None),
            P(row, col, None, None),
            P(row, col),
            P(row, col, None, None, None),
            P(),
            P(),
            P(),
            P(),
        ),
        out_specs=P(both, None),
        check_vma=False,
    )
```

```python
import functools

import jax
import jax.numpy as jnp
from jax import lax
from jax.experimental import pallas as pl
from jax.experimental.pallas import tpu as pltpu
from jax.sharding import Mesh, PartitionSpec as P

F32 = jnp.float32
BF16 = jnp.bfloat16
FLOOR = -1e30
BS = 128
HS = 256
EXT = 16
SRC = BS + EXT
ALL = SRC + BS
PER_DOT = 4


def split3(value):
    high = value.astype(BF16).astype(F32)
    rest = value - high
    middle = rest.astype(BF16).astype(F32)
    return high, middle, rest - middle


def pack_rows(value):
    high, middle, low = split3(jnp.broadcast_to(value, (EXT, BS)))
    row = lax.broadcasted_iota(jnp.int32, (EXT, BS), 0)
    zero = jnp.zeros_like(high)
    rows = jnp.where(row == 0, high, jnp.where(row == 1, middle, jnp.where(row == 2, low, zero)))
    return jnp.concatenate([rows, zero], axis=1).astype(BF16)


def unpack_rows(rows):
    wide = rows.astype(F32)
    return wide[0:1] + (wide[1:2] + wide[2:3])


def project_kernel(place, features, valid, attn, weight_src, weight_tgt, *outs):
    step = pl.program_id(0)
    source = jnp.dot(features[...], weight_src[...], preferred_element_type=F32).astype(BF16)
    target = jnp.dot(features[...], weight_tgt[...], preferred_element_type=F32).astype(BF16)
    linear = jnp.sum(
        source.astype(F32) * attn[pl.ds(step ^ place[0], 1), :], axis=1, keepdims=True
    )
    linear = jnp.broadcast_to(linear, (BS, BS)).T[0:1]
    extra = pack_rows(jnp.where(valid[...] > 0, linear, FLOOR))
    for d, out in enumerate(outs):

        @pl.when(step == d)
        def _():
            out[:BS, :] = source
            out[BS:SRC, :] = extra
            out[SRC:, :] = target


def project(place, features, valid, attn, weight_src, weight_tgt):
    heads = attn.shape[0]
    width = features.shape[1]
    return pl.pallas_call(
        project_kernel,
        grid_spec=pltpu.PrefetchScalarGridSpec(
            num_scalar_prefetch=1,
            grid=(heads,),
            in_specs=[
                pl.BlockSpec((BS, width), lambda d, place: (0, 0)),
                pl.BlockSpec((1, BS), lambda d, place: (0, 0)),
                pl.BlockSpec((heads, HS), lambda d, place: (0, 0)),
                pl.BlockSpec((width, HS), lambda d, place: (0, d ^ place[0])),
                pl.BlockSpec((width, HS), lambda d, place: (0, d ^ place[0])),
            ],
            out_specs=[pl.BlockSpec((ALL, HS), lambda d, place: (0, 0))] * heads,
        ),
        out_shape=[jax.ShapeDtypeStruct((ALL, HS), BF16)] * heads,
        name="project",
    )(place, features, valid, attn, weight_src, weight_tgt)


def gather_kernel(*refs):
    parts, (source, target) = refs[:4], refs[4:]
    for d, part in enumerate(parts):
        source[d] = part[:SRC, :]
        target[d] = part[SRC:, :]


def gather_square(parts):
    return pl.pallas_call(
        gather_kernel,
        out_shape=[
            jax.ShapeDtypeStruct((4, SRC, HS), BF16),
            jax.ShapeDtypeStruct((4, BS, HS), BF16),
        ],
        name="gather_square",
    )(*parts)


def pair_kernel(first, second, out):
    out[:4] = first[...]
    out[4:] = second[...]


def pair(first, second):
    return pl.pallas_call(
        pair_kernel, out_shape=jax.ShapeDtypeStruct((8, *first.shape[1:]), BF16), name="pair"
    )(first, second)


def score_plane(target, minus, wide, halves, scaled, planes):
    lane = lax.broadcasted_iota(jnp.int32, (BS, BS), 1)
    half = BS // 2
    wide[...] = target.astype(F32)
    tiled = wide[...].astype(BF16).reshape(BS // 16, 16, HS)
    weights = halves[...]
    left, right = scaled[:, :BS], scaled[:, BS:]
    waiting = []

    def flush():
        tiles = []
        for u, side in waiting:
            row = minus[u + side * half : u + side * half + 1, :]
            row = jnp.broadcast_to(row, (16, HS)).astype(BF16)
            tiles.append(jnp.maximum(tiled, row[None]).reshape(BS, HS))
        sums = jnp.dot(jnp.concatenate(tiles), weights, preferred_element_type=F32)
        for at, (u, side) in enumerate(waiting):
            pltpu.store(
                planes.at[side], sums[at * BS : (at + 1) * BS], mask=(lane == u) | (lane == u + half)
            )
        waiting.clear()

    for u in range(half):
        for side in range(2):
            if u % 2 == 0:
                waiting.append((u, side))
                if len(waiting) == PER_DOT:
                    flush()
            else:
                s = u + side * half
                row = minus[s : s + 1, :]
                terms = (
                    jnp.maximum(wide[:, :BS], row[:, :BS]) * left
                    + jnp.maximum(wide[:, BS:], row[:, BS:]) * right
                )
                sums = jnp.broadcast_to(jnp.sum(terms, axis=1, keepdims=True), (BS, BS))
                pltpu.store(planes.at[2], sums, mask=lane == s)
    low, high = planes[0], planes[1]
    low = low + pltpu.roll(low, half, 1)
    high = high + pltpu.roll(high, half, 1)
    return jnp.where(lane % 2 == 1, planes[2], jnp.where(lane < half, low, high))


def attend_kernel(kind, split, picked, shift, *refs):
    parts = split[2]
    if kind == "self":
        target_pieces, source_pieces, (masks, halves, scaled, *outs) = refs[:1], refs[1:2], refs[2:]
        outs, (acc, peak, den, minus, wide, planes) = outs[:parts], outs[parts:]
        targets, sources = target_pieces[0], source_pieces[0]
    else:
        count, target_at, source_at, out_at, pick_at, masks, halves, scaled = refs[:8]
        target_pieces, source_pieces = refs[8 : 8 + split[0]], refs[8 + split[0] : 8 + sum(split[:2])]
        rest = refs[8 + sum(split[:2]) :]
        outs, (acc, peak, den, minus, wide, planes, targets, sources, sems) = rest[:parts], rest[parts:]
    blocks = acc.shape[0]
    copies = []
    if kind != "self":
        for pieces, table in ((target_pieces, targets), (source_pieces, sources)):
            at = 0
            for piece in pieces:
                size = piece.shape[0]
                copies.append(
                    pltpu.make_async_copy(piece, table.at[pl.ds(at, size)], sems.at[len(copies)])
                )
                at += size
    for copy in copies:
        copy.start()

    def clear(b, carry):
        acc[b] = jnp.zeros((BS, HS), F32)
        peak[b] = jnp.full((BS, BS), FLOOR, F32)
        den[b] = jnp.zeros((BS, BS), F32)
        return carry

    lax.fori_loop(0, blocks, clear, 0, unroll=4)
    for copy in copies:
        copy.wait()

    def one(cell, slot, a, b, c):
        source = sources[b, :BS, :]
        minus[...] = -source.astype(F32)
        linear = unpack_rows(sources[b, BS:SRC, :BS])
        scores = score_plane(targets[a], minus, wide, halves, scaled[...], planes)
        mask = masks[cell, pl.ds(pl.multiple_of(slot * BS, BS), BS), :].astype(F32)
        if kind == "backward":
            mask = mask.T
        scores = jnp.where(mask > 0, scores + linear, FLOOR)
        before = peak[c]
        top = jnp.maximum(before, jnp.max(scores, axis=1, keepdims=True))
        scale = jnp.exp(before - top)
        weights = jnp.exp(scores - top)
        peak[c] = top
        den[c] = den[c] * scale + jnp.sum(weights, axis=1, keepdims=True)
        acc[c] = acc[c] * jnp.concatenate([scale, scale], axis=1) + jnp.dot(
            weights.astype(BF16), source, preferred_element_type=F32
        )

    if kind == "self":

        def own_step(b, carry):
            one(b, 8, b, b, b)
            return carry

        lax.fori_loop(0, blocks, own_step, 0)
    else:
        ends = [count[0], count[0] + count[1], count[0] + count[1] + count[2]]

        def step(i, carry):
            cell, start = jnp.int32(0), jnp.int32(0)
            for end in ends:
                past = i >= end
                cell = cell + jnp.where(past, 1, 0)
                start = jnp.where(past, end, start)
            slot = i - start
            at = cell * 8 + slot
            pick = pick_at[at]

            @pl.when((pick >= picked[0]) & (pick < picked[1]))
            def _():
                one(cell, slot, target_at[at] - shift, source_at[at], out_at[at] - shift)

            return carry

        lax.fori_loop(0, ends[2] + count[3], step, 0)

    each = blocks // parts
    for part, out in enumerate(outs):

        def finish(at, carry):
            b = part * each + at
            total = jnp.maximum(den[b], 1e-30)
            inverse = 1.0 / total
            out[at, :BS, :] = (acc[b] * jnp.concatenate([inverse, inverse], axis=1)).astype(BF16)
            out[at, BS:, :] = pack_rows((peak[b] + jnp.log(total)).T[0:1])
            return carry

        lax.fori_loop(0, each, finish, 0, unroll=4)


def attend(kind, lists, masks, attn, targets, sources, blocks=4, parts=1, picked=None, shift=0):
    smem = pl.BlockSpec(memory_space=pltpu.SMEM)
    vmem = pl.BlockSpec(memory_space=pltpu.VMEM)
    hbm = pl.BlockSpec(memory_space=pltpu.HBM)
    split = (len(targets), len(sources), parts)
    slots = 4 if kind == "self" else 8
    scratch = [
        pltpu.VMEM((blocks, BS, HS), F32),
        pltpu.VMEM((blocks, BS, BS), F32),
        pltpu.VMEM((blocks, BS, BS), F32),
        pltpu.VMEM((BS, HS), F32),
        pltpu.VMEM((BS, HS), F32),
        pltpu.VMEM((3, BS, BS), F32),
    ]
    if kind == "self":
        operands = (*targets, *sources, masks, *attn)
        specs = [vmem] * 5
    else:
        operands = (*lists, masks, *attn, *targets, *sources)
        specs = [smem] * 5 + [vmem] * 3 + [hbm] * sum(split[:2])
        scratch += [
            pltpu.VMEM((sum(t.shape[0] for t in targets), BS, HS), BF16),
            pltpu.VMEM((sum(t.shape[0] for t in sources), SRC, HS), BF16),
            pltpu.SemaphoreType.DMA((sum(split[:2]),)),
        ]
    return pl.pallas_call(
        functools.partial(attend_kernel, kind, split, picked, shift),
        out_shape=[jax.ShapeDtypeStruct((blocks // parts, SRC, HS), BF16)] * parts,
        in_specs=specs,
        out_specs=[vmem] * parts,
        scratch_shapes=scratch,
        compiler_params=pltpu.CompilerParams(
            vmem_limit_bytes=(16 if kind == "self" else 56) << 20
        ),
        cost_estimate=pl.CostEstimate(
            flops=slots * BS * BS * HS * 512, bytes_accessed=1 << 20, transcendentals=0
        ),
        name="attend_" + kind,
    )(*operands)


def merge_kernel(place, far, *refs):
    *single, bias = refs[:-4]
    outs = refs[-4:]
    step = pl.program_id(0)
    parts = [far.at[p, 0] for p in range(8)] + [ref.at[0] for ref in single]
    sums = [unpack_rows(part[BS:SRC, :BS]) for part in parts]
    top = functools.reduce(jnp.maximum, sums)
    shares = [jnp.exp(value - top) for value in sums]
    total = functools.reduce(jnp.add, shares)
    table = jnp.concatenate([share / total for share in shares] + [jnp.zeros((BS - len(parts), BS), F32)])
    table = table.T
    result = jnp.zeros((BS, HS), F32)
    for p, part in enumerate(parts):
        result = result + part[:BS, :].astype(F32) * table[:, p : p + 1]
    result = (result + bias[...]).astype(BF16)
    for d, out in enumerate(outs):

        @pl.when(step == d)
        def _():
            out[...] = result


def merge(place, far, single, bias):
    blocks = single[0].shape[0]
    return pl.pallas_call(
        merge_kernel,
        grid_spec=pltpu.PrefetchScalarGridSpec(
            num_scalar_prefetch=1,
            grid=(blocks,),
            in_specs=[pl.BlockSpec((8, 1, SRC, HS), lambda d, place: (0, d, 0, 0))]
            + [pl.BlockSpec((1, SRC, HS), lambda d, place: (d, 0, 0))] * len(single)
            + [pl.BlockSpec((1, HS), lambda d, place: (0, 0))],
            out_specs=[pl.BlockSpec((BS, HS), lambda d, place: (0, 0))] * blocks,
        ),
        out_shape=[jax.ShapeDtypeStruct((BS, HS), BF16)] * blocks,
        name="merge",
    )(place, far, *single, bias)


def finish_kernel(place, valid, bias, *refs):
    *parts, out = refs
    flags = jnp.broadcast_to(valid[...].astype(F32), (BS, BS)).T[:, 0:1]
    for d, part in enumerate(parts):
        at = pl.multiple_of((place[0] ^ d) * HS, HS)
        row = bias[:, pl.ds(at, HS)]
        kept = jnp.where(flags > 0, part[...].astype(F32), row)
        out[:, pl.ds(at, HS)] = kept.astype(BF16)


def finish_rows(place, valid, bias, parts):
    smem = pl.BlockSpec(memory_space=pltpu.SMEM)
    vmem = pl.BlockSpec(memory_space=pltpu.VMEM)
    return pl.pallas_call(
        finish_kernel,
        out_shape=jax.ShapeDtypeStruct((BS, HS * len(parts)), BF16),
        in_specs=[smem] + [vmem] * (2 + len(parts)),
        out_specs=vmem,
        name="finish_rows",
    )(place, valid, bias, *parts)


def body(
    features,
    node_valid,
    self_mask,
    pair_blocks,
    pair_count,
    pair_masks,
    weight_src,
    weight_tgt,
    attn,
    bias,
):
    heads = attn.shape[0]
    group = ("rp", "cp")
    row_part, col_part = lax.axis_index("rp"), lax.axis_index("cp")
    head = row_part * 2 + col_part

    place = head.reshape(1)

    def swap(d, value):
        return lax.ppermute(value, group, [(i, i ^ d) for i in range(4)])

    sent = project(place, features, node_valid, attn, weight_src, weight_tgt)
    mine = [sent[0]] + [swap(d, sent[d]) for d in (1, 2, 3)]

    identity = jnp.eye(BS, dtype=bool)
    own_mask = (self_mask[0] > 0) | identity
    first, second = pair_blocks[0, 0, :, 0] % 16, pair_blocks[0, 0, :, 1] // 16
    first_at = (first // 2) * 4 + row_part * 2 + first % 2
    second_at = (second // 2) * 4 + (second % 2) * 2 + col_part
    info = jnp.stack([first_at, second_at, jnp.broadcast_to(pair_count[0, 0], (8,))])
    info = jnp.pad(info, ((0, EXT - 3), (0, BS - 8)))
    cell = jnp.concatenate(
        [
            pair_masks.reshape(8 * BS, BS).astype(BF16),
            own_mask.astype(BF16),
            info.astype(BF16),
        ]
    )
    cells = jnp.stack([cell] + [swap(d, cell) for d in (1, 2, 3)])
    lists = cells[:, 9 * BS : 9 * BS + 3, :8].astype(jnp.int32)
    first_at, second_at = lists[:, 0].reshape(32) ^ head, lists[:, 1].reshape(32) ^ head
    count = lists[:, 2, 0]
    me = lax.axis_index("R")
    from_row = second_at // 4
    y_steps = (me // 2 - from_row // 2) % 4
    x_steps = (me + from_row) % 2
    second_near = ((y_steps + 3) % 4 * 2 + x_steps) * 4 + second_at % 4

    source, target = gather_square(mine)

    size = lax.axis_size("R")
    across = [(i, i ^ 1) for i in range(size)]
    around = [[(i, (i + 2 * k) % size) for i in range(size)] for k in (1, 2, 3)]

    row_targets = lax.all_gather(target, "C", axis=0, tiled=True)
    source_beside = lax.ppermute(source, "R", across)
    source_beside, later_target = lax.optimization_barrier((source_beside, target))
    col_sources = []
    for way in around:
        col_sources += [lax.ppermute(source, "R", way), lax.ppermute(source_beside, "R", way)]
    col_sources += [source, source_beside]
    target_beside = lax.ppermute(later_target, "R", across)

    scaled = 0.8 * lax.dynamic_index_in_dim(attn, head, 0, keepdims=False)
    high = lax.reduce_precision(scaled, 8, 7)
    low = scaled - high
    halves = jnp.concatenate(
        [jnp.broadcast_to(part[:, None], (HS, BS // 2)) for part in (high, low)], axis=1
    ).astype(BF16)
    shared = (halves, scaled[None])

    both = pair(later_target, target_beside)
    lists = (count, first_at, second_near, second_at)
    row_targets, both, later_source, col_sources, cells, shared, lists = lax.optimization_barrier(
        (row_targets, both, source, col_sources, cells, shared, lists)
    )
    count, first_at, second_near, second_at = lists
    row_sources = lax.all_gather(later_source, "C", axis=0, tiled=True)
    around_targets = [lax.ppermute(both, "R", way) for way in around]
    (to_far,) = attend(
        "forward",
        (count, first_at, second_near, first_at, first_at),
        cells,
        shared,
        [row_targets],
        col_sources,
        blocks=32,
        picked=(0, 32),
    )
    to_far, around_targets = lax.optimization_barrier((to_far, around_targets))
    far = lax.all_to_all(to_far, "C", 0, 0, tiled=True).reshape(8, 4, SRC, HS)
    cols, column_targets = [], [around_targets[:2], [around_targets[2], both]]
    for half in range(2):
        to_cols = attend(
            "backward",
            (count, second_near, first_at, second_near, second_near),
            cells,
            shared,
            column_targets[half],
            [row_sources],
            blocks=16,
            parts=4,
            picked=(16 * half, 16 * half + 16),
            shift=16 * half,
        )
        to_cols, cols, column_targets[1] = lax.optimization_barrier(
            (to_cols, cols, column_targets[1])
        )
        for part, value in enumerate(to_cols):
            y_step, x_step = (1, 2, 3, 0)[half * 2 + part // 2], part % 2
            back = [(i, (i // 2 - y_step) % 4 * 2 + (i % 2 ^ x_step)) for i in range(size)]
            cols.append(value if y_step == x_step == 0 else lax.ppermute(value, "R", back))
    target, to_cols = lax.optimization_barrier((target, to_cols))
    (own,) = attend("self", (), cells, shared, [target], [source])
    bias_head = lax.dynamic_index_in_dim(bias.reshape(heads, HS), head, 0)
    merged = merge(place, far, [*cols, own], bias_head)
    parts = [merged[0]] + [swap(d, merged[d]) for d in (1, 2, 3)]
    return finish_rows(place, node_valid, bias[None], parts)


def solution(mesh):
    fine = Mesh(mesh.devices.reshape(8, 2, 8, 2), ("R", "rp", "C", "cp"))
    row, col = ("R", "rp"), ("C", "cp")
    both = row + col
    return jax.shard_map(
        body,
        mesh=fine,
        in_specs=(
            P(both, None),
            P(both, None),
            P(both, None, None),
            P(row, col, None, None),
            P(row, col),
            P(row, col, None, None, None),
            P(),
            P(),
            P(),
            P(),
        ),
        out_specs=P(both, None),
        check_vma=False,
    )
```

```python
import functools

import jax
import jax.numpy as jnp
from jax import lax
from jax.experimental import pallas as pl
from jax.experimental.pallas import tpu as pltpu
from jax.sharding import Mesh, PartitionSpec as P

F32 = jnp.float32
BF16 = jnp.bfloat16
FLOOR = -1e30
BS = 128
HS = 256
EXT = 16
SRC = BS + EXT
ALL = SRC + BS
PER_DOT = 4


def split3(value):
    high = value.astype(BF16).astype(F32)
    rest = value - high
    middle = rest.astype(BF16).astype(F32)
    return high, middle, rest - middle


def pack_rows(value):
    high, middle, low = split3(jnp.broadcast_to(value, (EXT, BS)))
    row = lax.broadcasted_iota(jnp.int32, (EXT, BS), 0)
    zero = jnp.zeros_like(high)
    rows = jnp.where(row == 0, high, jnp.where(row == 1, middle, jnp.where(row == 2, low, zero)))
    return jnp.concatenate([rows, zero], axis=1).astype(BF16)


def unpack_rows(rows):
    wide = rows.astype(F32)
    return wide[0:1] + (wide[1:2] + wide[2:3])


def project_kernel(place, features, valid, attn, weight_src, weight_tgt, *outs):
    step = pl.program_id(0)
    source = jnp.dot(features[...], weight_src[...], preferred_element_type=F32).astype(BF16)
    target = jnp.dot(features[...], weight_tgt[...], preferred_element_type=F32).astype(BF16)
    linear = jnp.sum(
        source.astype(F32) * attn[pl.ds(step ^ place[0], 1), :], axis=1, keepdims=True
    )
    linear = jnp.broadcast_to(linear, (BS, BS)).T[0:1]
    extra = pack_rows(jnp.where(valid[...] > 0, linear, FLOOR))
    for d, out in enumerate(outs):

        @pl.when(step == d)
        def _():
            out[:BS, :] = source
            out[BS:SRC, :] = extra
            out[SRC:, :] = target


def project(place, features, valid, attn, weight_src, weight_tgt):
    heads = attn.shape[0]
    width = features.shape[1]
    return pl.pallas_call(
        project_kernel,
        grid_spec=pltpu.PrefetchScalarGridSpec(
            num_scalar_prefetch=1,
            grid=(heads,),
            in_specs=[
                pl.BlockSpec((BS, width), lambda d, place: (0, 0)),
                pl.BlockSpec((1, BS), lambda d, place: (0, 0)),
                pl.BlockSpec((heads, HS), lambda d, place: (0, 0)),
                pl.BlockSpec((width, HS), lambda d, place: (0, d ^ place[0])),
                pl.BlockSpec((width, HS), lambda d, place: (0, d ^ place[0])),
            ],
            out_specs=[pl.BlockSpec((ALL, HS), lambda d, place: (0, 0))] * heads,
        ),
        out_shape=[jax.ShapeDtypeStruct((ALL, HS), BF16)] * heads,
        name="project",
    )(place, features, valid, attn, weight_src, weight_tgt)


def gather_kernel(*refs):
    parts, (source, target) = refs[:4], refs[4:]
    for d, part in enumerate(parts):
        source[d] = part[:SRC, :]
        target[d] = part[SRC:, :]


def gather_square(parts):
    return pl.pallas_call(
        gather_kernel,
        out_shape=[
            jax.ShapeDtypeStruct((4, SRC, HS), BF16),
            jax.ShapeDtypeStruct((4, BS, HS), BF16),
        ],
        name="gather_square",
    )(*parts)


def pair_kernel(first, second, out):
    out[:4] = first[...]
    out[4:] = second[...]


def pair(first, second):
    return pl.pallas_call(
        pair_kernel, out_shape=jax.ShapeDtypeStruct((8, *first.shape[1:]), BF16), name="pair"
    )(first, second)


def score_plane(target, minus, wide, halves, scaled, planes):
    lane = lax.broadcasted_iota(jnp.int32, (BS, BS), 1)
    half = BS // 2
    wide[...] = target.astype(F32)
    tiled = wide[...].astype(BF16).reshape(BS // 16, 16, HS)
    weights = halves[...]
    left, right = scaled[:, :BS], scaled[:, BS:]
    waiting = []

    def flush():
        tiles = []
        for u, side in waiting:
            row = minus[u + side * half : u + side * half + 1, :]
            row = jnp.broadcast_to(row, (16, HS)).astype(BF16)
            tiles.append(jnp.maximum(tiled, row[None]).reshape(BS, HS))
        sums = jnp.dot(jnp.concatenate(tiles), weights, preferred_element_type=F32)
        for at, (u, side) in enumerate(waiting):
            pltpu.store(
                planes.at[side], sums[at * BS : (at + 1) * BS], mask=(lane == u) | (lane == u + half)
            )
        waiting.clear()

    for u in range(half):
        for side in range(2):
            if u % 2 == 0:
                waiting.append((u, side))
                if len(waiting) == PER_DOT:
                    flush()
            else:
                s = u + side * half
                row = minus[s : s + 1, :]
                terms = (
                    jnp.maximum(wide[:, :BS], row[:, :BS]) * left
                    + jnp.maximum(wide[:, BS:], row[:, BS:]) * right
                )
                sums = jnp.broadcast_to(jnp.sum(terms, axis=1, keepdims=True), (BS, BS))
                pltpu.store(planes.at[2], sums, mask=lane == s)
    low, high = planes[0], planes[1]
    low = low + pltpu.roll(low, half, 1)
    high = high + pltpu.roll(high, half, 1)
    return jnp.where(lane % 2 == 1, planes[2], jnp.where(lane < half, low, high))


def attend_kernel(kind, split, picked, shift, *refs):
    parts = split[2]
    if kind == "self":
        target_pieces, source_pieces, (masks, halves, scaled, *outs) = refs[:1], refs[1:2], refs[2:]
        outs, (acc, peak, den, minus, wide, planes) = outs[:parts], outs[parts:]
        targets, sources = target_pieces[0], source_pieces[0]
    else:
        count, target_at, source_at, out_at, pick_at, masks, halves, scaled = refs[:8]
        target_pieces, source_pieces = refs[8 : 8 + split[0]], refs[8 + split[0] : 8 + sum(split[:2])]
        rest = refs[8 + sum(split[:2]) :]
        outs, (acc, peak, den, minus, wide, planes, targets, sources, sems) = rest[:parts], rest[parts:]
    blocks = acc.shape[0]
    copies = []
    if kind != "self":
        for pieces, table in ((target_pieces, targets), (source_pieces, sources)):
            at = 0
            for piece in pieces:
                size = piece.shape[0]
                copies.append(
                    pltpu.make_async_copy(piece, table.at[pl.ds(at, size)], sems.at[len(copies)])
                )
                at += size
    for copy in copies:
        copy.start()

    def clear(b, carry):
        acc[b] = jnp.zeros((BS, HS), F32)
        peak[b] = jnp.full((BS, BS), FLOOR, F32)
        den[b] = jnp.zeros((BS, BS), F32)
        return carry

    lax.fori_loop(0, blocks, clear, 0, unroll=4)
    for copy in copies:
        copy.wait()

    def one(cell, slot, a, b, c):
        source = sources[b, :BS, :]
        minus[...] = -source.astype(F32)
        linear = unpack_rows(sources[b, BS:SRC, :BS])
        scores = score_plane(targets[a], minus, wide, halves, scaled[...], planes)
        mask = masks[cell, pl.ds(pl.multiple_of(slot * BS, BS), BS), :].astype(F32)
        if kind == "backward":
            mask = mask.T
        scores = jnp.where(mask > 0, scores + linear, FLOOR)
        before = peak[c]
        top = jnp.maximum(before, jnp.max(scores, axis=1, keepdims=True))
        scale = jnp.exp(before - top)
        weights = jnp.exp(scores - top)
        peak[c] = top
        den[c] = den[c] * scale + jnp.sum(weights, axis=1, keepdims=True)
        acc[c] = acc[c] * jnp.concatenate([scale, scale], axis=1) + jnp.dot(
            weights.astype(BF16), source, preferred_element_type=F32
        )

    if kind == "self":

        def own_step(b, carry):
            one(b, 8, b, b, b)
            return carry

        lax.fori_loop(0, blocks, own_step, 0)
    else:
        ends = [count[0], count[0] + count[1], count[0] + count[1] + count[2]]

        def step(i, carry):
            cell, start = jnp.int32(0), jnp.int32(0)
            for end in ends:
                past = i >= end
                cell = cell + jnp.where(past, 1, 0)
                start = jnp.where(past, end, start)
            slot = i - start
            at = cell * 8 + slot
            pick = pick_at[at]

            @pl.when((pick >= picked[0]) & (pick < picked[1]))
            def _():
                one(cell, slot, target_at[at] - shift, source_at[at], out_at[at] - shift)

            return carry

        lax.fori_loop(0, ends[2] + count[3], step, 0)

    each = blocks // parts
    for part, out in enumerate(outs):

        def finish(at, carry):
            b = part * each + at
            total = jnp.maximum(den[b], 1e-30)
            inverse = 1.0 / total
            out[at, :BS, :] = (acc[b] * jnp.concatenate([inverse, inverse], axis=1)).astype(BF16)
            out[at, BS:, :] = pack_rows((peak[b] + jnp.log(total)).T[0:1])
            return carry

        lax.fori_loop(0, each, finish, 0, unroll=4)


def attend(kind, lists, masks, attn, targets, sources, blocks=4, parts=1, picked=None, shift=0):
    smem = pl.BlockSpec(memory_space=pltpu.SMEM)
    vmem = pl.BlockSpec(memory_space=pltpu.VMEM)
    hbm = pl.BlockSpec(memory_space=pltpu.HBM)
    split = (len(targets), len(sources), parts)
    slots = 4 if kind == "self" else 8
    scratch = [
        pltpu.VMEM((blocks, BS, HS), F32),
        pltpu.VMEM((blocks, BS, BS), F32),
        pltpu.VMEM((blocks, BS, BS), F32),
        pltpu.VMEM((BS, HS), F32),
        pltpu.VMEM((BS, HS), F32),
        pltpu.VMEM((3, BS, BS), F32),
    ]
    if kind == "self":
        operands = (*targets, *sources, masks, *attn)
        specs = [vmem] * 5
    else:
        operands = (*lists, masks, *attn, *targets, *sources)
        specs = [smem] * 5 + [vmem] * 3 + [hbm] * sum(split[:2])
        scratch += [
            pltpu.VMEM((sum(t.shape[0] for t in targets), BS, HS), BF16),
            pltpu.VMEM((sum(t.shape[0] for t in sources), SRC, HS), BF16),
            pltpu.SemaphoreType.DMA((sum(split[:2]),)),
        ]
    return pl.pallas_call(
        functools.partial(attend_kernel, kind, split, picked, shift),
        out_shape=[jax.ShapeDtypeStruct((blocks // parts, SRC, HS), BF16)] * parts,
        in_specs=specs,
        out_specs=[vmem] * parts,
        scratch_shapes=scratch,
        compiler_params=pltpu.CompilerParams(
            vmem_limit_bytes=(16 if kind == "self" else 56) << 20
        ),
        cost_estimate=pl.CostEstimate(
            flops=slots * BS * BS * HS * 512, bytes_accessed=1 << 20, transcendentals=0
        ),
        name="attend_" + kind,
    )(*operands)


def merge_kernel(place, far, *refs):
    *single, bias = refs[:-4]
    outs = refs[-4:]
    step = pl.program_id(0)
    parts = [far.at[p, 0] for p in range(8)] + [ref.at[0] for ref in single]
    sums = [unpack_rows(part[BS:SRC, :BS]) for part in parts]
    top = functools.reduce(jnp.maximum, sums)
    shares = [jnp.exp(value - top) for value in sums]
    total = functools.reduce(jnp.add, shares)
    table = jnp.concatenate([share / total for share in shares] + [jnp.zeros((BS - len(parts), BS), F32)])
    table = table.T
    result = jnp.zeros((BS, HS), F32)
    for p, part in enumerate(parts):
        result = result + part[:BS, :].astype(F32) * table[:, p : p + 1]
    result = (result + bias[...]).astype(BF16)
    for d, out in enumerate(outs):

        @pl.when(step == d)
        def _():
            out[...] = result


def merge(place, far, single, bias):
    blocks = single[0].shape[0]
    return pl.pallas_call(
        merge_kernel,
        grid_spec=pltpu.PrefetchScalarGridSpec(
            num_scalar_prefetch=1,
            grid=(blocks,),
            in_specs=[pl.BlockSpec((8, 1, SRC, HS), lambda d, place: (0, d, 0, 0))]
            + [pl.BlockSpec((1, SRC, HS), lambda d, place: (d, 0, 0))] * len(single)
            + [pl.BlockSpec((1, HS), lambda d, place: (0, 0))],
            out_specs=[pl.BlockSpec((BS, HS), lambda d, place: (0, 0))] * blocks,
        ),
        out_shape=[jax.ShapeDtypeStruct((BS, HS), BF16)] * blocks,
        name="merge",
    )(place, far, *single, bias)


def finish_kernel(place, valid, bias, *refs):
    *parts, out = refs
    flags = jnp.broadcast_to(valid[...].astype(F32), (BS, BS)).T[:, 0:1]
    for d, part in enumerate(parts):
        at = pl.multiple_of((place[0] ^ d) * HS, HS)
        row = bias[:, pl.ds(at, HS)]
        kept = jnp.where(flags > 0, part[...].astype(F32), row)
        out[:, pl.ds(at, HS)] = kept.astype(BF16)


def finish_rows(place, valid, bias, parts):
    smem = pl.BlockSpec(memory_space=pltpu.SMEM)
    vmem = pl.BlockSpec(memory_space=pltpu.VMEM)
    return pl.pallas_call(
        finish_kernel,
        out_shape=jax.ShapeDtypeStruct((BS, HS * len(parts)), BF16),
        in_specs=[smem] + [vmem] * (2 + len(parts)),
        out_specs=vmem,
        name="finish_rows",
    )(place, valid, bias, *parts)


def body(
    features,
    node_valid,
    self_mask,
    pair_blocks,
    pair_count,
    pair_masks,
    weight_src,
    weight_tgt,
    attn,
    bias,
):
    heads = attn.shape[0]
    group = ("rp", "cp")
    row_part, col_part = lax.axis_index("rp"), lax.axis_index("cp")
    head = row_part * 2 + col_part

    place = head.reshape(1)

    def swap(d, value):
        return lax.ppermute(value, group, [(i, i ^ d) for i in range(4)])

    sent = project(place, features, node_valid, attn, weight_src, weight_tgt)
    sent, pair_masks = lax.optimization_barrier((sent, pair_masks))
    mine = [sent[0]] + [swap(d, sent[d]) for d in (1, 2, 3)]

    identity = jnp.eye(BS, dtype=bool)
    own_mask = (self_mask[0] > 0) | identity
    first, second = pair_blocks[0, 0, :, 0] % 16, pair_blocks[0, 0, :, 1] // 16
    first_at = (first // 2) * 4 + row_part * 2 + first % 2
    second_at = (second // 2) * 4 + (second % 2) * 2 + col_part
    info = jnp.stack([first_at, second_at, jnp.broadcast_to(pair_count[0, 0], (8,))])
    info = jnp.pad(info, ((0, EXT - 3), (0, BS - 8)))
    cell = jnp.concatenate(
        [
            pair_masks.reshape(8 * BS, BS).astype(BF16),
            own_mask.astype(BF16),
            info.astype(BF16),
        ]
    )
    swapped = [cell] + [swap(d, cell) for d in (1, 2, 3)]
    mine[0], swapped[2] = lax.optimization_barrier((mine[0], swapped[2]))
    cells = jnp.stack(swapped)
    lists = cells[:, 9 * BS : 9 * BS + 3, :8].astype(jnp.int32)
    first_at, second_at = lists[:, 0].reshape(32) ^ head, lists[:, 1].reshape(32) ^ head
    count = lists[:, 2, 0]
    me = lax.axis_index("R")
    from_row = second_at // 4
    y_steps = (me // 2 - from_row // 2) % 4
    x_steps = (me + from_row) % 2
    second_near = ((y_steps + 3) % 4 * 2 + x_steps) * 4 + second_at % 4

    source, target = gather_square(mine)

    size = lax.axis_size("R")
    across = [(i, i ^ 1) for i in range(size)]
    around = [[(i, (i + 2 * k) % size) for i in range(size)] for k in (1, 2, 3)]

    row_targets = lax.all_gather(target, "C", axis=0, tiled=True)
    source_beside = lax.ppermute(source, "R", across)
    source_beside, later_target = lax.optimization_barrier((source_beside, target))
    col_sources = []
    for way in around:
        col_sources += [lax.ppermute(source, "R", way), lax.ppermute(source_beside, "R", way)]
    col_sources += [source, source_beside]
    target_beside = lax.ppermute(later_target, "R", across)

    scaled = 0.8 * lax.dynamic_index_in_dim(attn, head, 0, keepdims=False)
    high = lax.reduce_precision(scaled, 8, 7)
    low = scaled - high
    halves = jnp.concatenate(
        [jnp.broadcast_to(part[:, None], (HS, BS // 2)) for part in (high, low)], axis=1
    ).astype(BF16)
    shared = (halves, scaled[None])

    both = pair(later_target, target_beside)
    lists = (count, first_at, second_near, second_at)
    row_targets, both, later_source, col_sources, cells, shared, lists = lax.optimization_barrier(
        (row_targets, both, source, col_sources, cells, shared, lists)
    )
    count, first_at, second_near, second_at = lists
    row_sources = lax.all_gather(later_source, "C", axis=0, tiled=True)
    around_targets = [lax.ppermute(both, "R", way) for way in around]
    (to_far,) = attend(
        "forward",
        (count, first_at, second_near, first_at, first_at),
        cells,
        shared,
        [row_targets],
        col_sources,
        blocks=32,
        picked=(0, 32),
    )
    to_far, around_targets = lax.optimization_barrier((to_far, around_targets))
    far = lax.all_to_all(to_far, "C", 0, 0, tiled=True).reshape(8, 4, SRC, HS)
    cols, column_targets = [], [around_targets[:2], [around_targets[2], both]]
    for half in range(2):
        to_cols = attend(
            "backward",
            (count, second_near, first_at, second_near, second_near),
            cells,
            shared,
            column_targets[half],
            [row_sources],
            blocks=16,
            parts=4,
            picked=(16 * half, 16 * half + 16),
            shift=16 * half,
        )
        to_cols, cols, column_targets[1] = lax.optimization_barrier(
            (to_cols, cols, column_targets[1])
        )
        for part, value in enumerate(to_cols):
            y_step, x_step = (1, 2, 3, 0)[half * 2 + part // 2], part % 2
            back = [(i, (i // 2 - y_step) % 4 * 2 + (i % 2 ^ x_step)) for i in range(size)]
            cols.append(value if y_step == x_step == 0 else lax.ppermute(value, "R", back))
    target, to_cols = lax.optimization_barrier((target, to_cols))
    (own,) = attend("self", (), cells, shared, [target], [source])
    bias_head = lax.dynamic_index_in_dim(bias.reshape(heads, HS), head, 0)
    merged = merge(place, far, [*cols, own], bias_head)
    parts = [merged[0]] + [swap(d, merged[d]) for d in (1, 2, 3)]
    return finish_rows(place, node_valid, bias[None], parts)


def solution(mesh):
    fine = Mesh(mesh.devices.reshape(8, 2, 8, 2), ("R", "rp", "C", "cp"))
    row, col = ("R", "rp"), ("C", "cp")
    both = row + col
    return jax.shard_map(
        body,
        mesh=fine,
        in_specs=(
            P(both, None),
            P(both, None),
            P(both, None, None),
            P(row, col, None, None),
            P(row, col),
            P(row, col, None, None, None),
            P(),
            P(),
            P(),
            P(),
        ),
        out_specs=P(both, None),
        check_vma=False,
    )
```
